32 devices in a mesh: rows: 8 (over y, x, core), fields: 4 (over z).
Axes of the slice: x: 2, y: 2, z: 4, core: 2. Of those that a mesh axis runs over, the one named last changes fastest.
Arguments:
- deviation: float32 [64, 3, 128, 2048], P('fields', None, 'rows'), may hold values from -5.5 to 5.5
- seeds: int32 [64], P('fields'), may hold values from 0 to 1048575
- velocity: float32 [2, 128, 2048], P(None, 'rows'), may hold values from -5.5 to 5.5
- forcing: float32 [2, 128, 2048], P(None, 'rows'), may hold values from -6 to 6
Outputs:
- new_deviation: float32 [64, 3, 128, 2048], P('fields', None, 'rows')
- new_velocity: float32 [2, 128, 2048], P(None, 'rows')
The draws below stay inside these ranges and needn't reach their ends.
All inputs are finite; a program needn't handle non-finite values. Where the reference program divides by a largest or mean magnitude, that divisor is 1e-20 or more.
Results may differ from the reference program's by a relative error of at most 0.0003.
Values sent between devices are 32-bit elements; how exact they have to be, the bound alone decides.
A program may use at most 64 MiB of HBM per device.

```python
import jax
import jax.numpy as jnp
from jax import lax

FIELDS = 64
NY = 2048
SWEEPS = 8
STEPS = 2
NX = 128


def draw_forcing(key, part):
    row_pos = jnp.arange(NX, dtype=jnp.float32) / NX
    ramp = (1.0 + 2.0 * row_pos)[None, :, None]
    base = jnp.clip(jax.random.normal(key, (2, NX, NY), jnp.float32), -4.0, 4.0)
    return ramp * 0.5 * base


def draw_deviation(key, part):
    row_pos = jnp.arange(NX, dtype=jnp.float32) / NX
    ramp = 1.0 + 2.0 * row_pos
    offset = jax.random.randint(jax.random.fold_in(key, 11), (), 0, 4)
    phase = (jnp.arange(NX, dtype=jnp.int32) + offset) % 4
    pattern = jnp.where(phase < 2, 1.0, -1.0).astype(jnp.float32)
    factors = jax.random.uniform(jax.random.fold_in(key, 12), (FIELDS,), jnp.float32, 0.5, 1.5)
    shared = factors[:, None, None, None] * (ramp * pattern)[None, None, :, None]
    comp_mask = jnp.array([0.0, 1.0, 0.0], jnp.float32)[None, :, None, None]
    base = 0.5 * jnp.clip(jax.random.normal(key, (FIELDS, 3, NX, NY), jnp.float32), -2.0, 2.0)
    return base + 0.8 * comp_mask * shared


def draw_velocity(key, part):
    row_pos = jnp.arange(NX, dtype=jnp.float32) / NX
    ramp = (1.0 + 2.0 * row_pos)[None, :, None]
    parity = (jnp.arange(NX, dtype=jnp.int32)[:, None] + jnp.arange(NY, dtype=jnp.int32)[None, :]) % 2
    checker = jnp.where(parity == 0, 1.0, -1.0).astype(jnp.float32)[None]
    signs = (2 * jax.random.randint(jax.random.fold_in(key, 21), (2,), 0, 2) - 1).astype(jnp.float32)[:, None, None]
    base = 0.25 * jnp.clip(jax.random.normal(key, (2, NX, NY), jnp.float32), -2.0, 2.0)
    return ramp * (1.2 * signs * checker + base)


def set_ends(values, stream_key, smallest, high):
    spot = [jax.random.randint(jax.random.fold_in(stream_key, axis), (), 0, length) for axis, length in enumerate(values.shape)]
    longest = values.shape.index(max(values.shape))
    next_to = spot[:longest] + [(spot[longest] + 1) % values.shape[longest]] + spot[longest + 1:]
    return values.at[tuple(spot)].set(smallest).at[tuple(next_to)].set(high)


def setup_inputs(seed: int = 0) -> dict:
    key_of = jax.random.split(jax.random.key(seed), 5)
    return {
        "deviation": draw_deviation(jax.random.fold_in(key_of[4], 71), 0),
        "seeds": set_ends(jax.random.randint(key_of[1], (FIELDS,), 0, 1048576), jax.random.fold_in(key_of[1], 1), 0, 1048575).astype(jnp.int32),
        "velocity": draw_velocity(jax.random.fold_in(key_of[4], 71), 0),
        "forcing": draw_forcing(jax.random.fold_in(key_of[4], 71), 0),
    }


G_COEF = 4.0
ALPHA = 0.05
LMAX2 = 20.0
LAMBDA = 1.0
DT = 0.2
SIGMA = 1.0

def periodic_rows(values, width):
    return jnp.concatenate([values[..., -width:, :], values, values[..., :width, :]], axis=-2)

def ddx(values):
    return (jnp.roll(values, -1, axis=-1) - jnp.roll(values, 1, axis=-1)) * 0.5

def ddy(values):
    return (values[..., 2:, :] - values[..., :-2, :]) * 0.5

def divergence(tensor):
    fx = ddx(tensor[0, 1:-1]) + ddy(tensor[1])
    fy = ddx(tensor[1, 1:-1]) + ddy(tensor[2])
    return jnp.stack([fx, fy])

def relax(padded, rhs):
    middle = padded[:, 1:-1]
    beside_all = padded[:, 2:] + padded[:, :-2] + jnp.roll(middle, -1, axis=-1) + jnp.roll(middle, 1, axis=-1)
    return (rhs + beside_all) / (ALPHA + 4.0)

def scramble(hashed):
    hashed = jnp.bitwise_xor(hashed, lax.shift_right_logical(hashed, jnp.int32(16)))
    hashed = hashed * jnp.int32(73244475)
    hashed = jnp.bitwise_xor(hashed, lax.shift_right_logical(hashed, jnp.int32(16)))
    hashed = hashed * jnp.int32(73244475)
    hashed = jnp.bitwise_xor(hashed, lax.shift_right_logical(hashed, jnp.int32(16)))
    return hashed

def make_noise(seed_block, step, row_start, row_count, width):
    row_ids = (row_start + jnp.arange(row_count, dtype=jnp.int32)).astype(jnp.int32)
    cell_ids = row_ids[:, None] * jnp.int32(width) + jnp.arange(width, dtype=jnp.int32)[None, :]
    comps = jnp.arange(3, dtype=jnp.int32)
    hashed = seed_block[:, None, None, None] * jnp.int32(2654435) + ((3 * step + comps) * 97531).astype(jnp.int32)[None, :, None, None] + cell_ids[None, None]
    hashed = scramble(hashed.astype(jnp.int32))
    return (jnp.bitwise_and(hashed, jnp.int32(65535)).astype(jnp.float32) - 32767.5) / 18918.6

def advance(extended, seed_block, speed_x, speed_y, grads, dt, step, row_start):
    inner = extended[:, :, 1:-1]
    west = jnp.roll(inner, 1, axis=-1)
    east = jnp.roll(inner, -1, axis=-1)
    south = extended[:, :, :-2]
    north = extended[:, :, 2:]
    advect = jnp.maximum(speed_x, 0.0) * (inner - west) + jnp.minimum(speed_x, 0.0) * (east - inner) + jnp.maximum(speed_y, 0.0) * (inner - south) + jnp.minimum(speed_y, 0.0) * (north - inner)
    lxx, lxy, lyx, lyy = grads
    comp_a, comp_b, comp_c = (inner[:, 0], inner[:, 1], inner[:, 2])
    stretch = jnp.stack([2.0 * lxx + 2.0 * (lxx * comp_a + lxy * comp_b), lxy + lyx + lxx * comp_b + lxy * comp_c + lyx * comp_a + lyy * comp_b, 2.0 * lyy + 2.0 * (lyx * comp_b + lyy * comp_c)], axis=1)
    spring = 1.0 + (2.0 + comp_a + comp_c) / LMAX2
    noise = make_noise(seed_block, step, row_start, inner.shape[2], inner.shape[3])
    return inner + dt * (stretch - advect - spring[:, None] * inner / LAMBDA) + jnp.sqrt(dt) * SIGMA * noise

def reference(deviation, seeds, velocity, forcing):
    field_now = deviation
    speed_now = velocity
    for step in range(STEPS):
        extended = periodic_rows(field_now, 1)

        def add_field(total, one):
            spring = 1.0 + (2.0 + one[0] + one[2]) / LMAX2
            return (total + spring[None] * one, None)
        start = jnp.zeros((3, extended.shape[2], extended.shape[3]), jnp.float32)
        total, _ = lax.scan(add_field, start, extended)
        stress = G_COEF / FIELDS * total
        rhs = forcing + divergence(stress)
        for sweep in range(SWEEPS):
            speed_now = relax(periodic_rows(speed_now, 1), rhs)
        rim = periodic_rows(speed_now, 1)
        grads = (ddx(speed_now[0]), ddy(rim[0]), ddx(speed_now[1]), ddy(rim[1]))
        largest = jnp.max(jnp.abs(speed_now[0]) + jnp.abs(speed_now[1]))
        dt = DT / (1.0 + largest)

        def one_field(pair):
            ext_one, seed_one = pair
            return advance(ext_one[None], seed_one[None], speed_now[0], speed_now[1], grads, dt, step, 0)[0]
        field_now = lax.map(one_field, (extended, seeds))
    return (field_now, speed_now)
```

```python
import functools

import jax
import jax.numpy as jnp
from jax import lax
from jax.experimental import pallas as pl
from jax.experimental.pallas import tpu as pltpu
from jax.sharding import PartitionSpec as P

FIELDS = 64
SWEEPS = 8
STEPS = 2

G_COEF = 4.0
ALPHA = 0.05
LMAX2 = 20.0
LAMBDA = 1.0
DT = 0.2
SIGMA = 1.0

K = 8
LAG = 2
MESH = pl.DeviceIdType.MESH


def widened(load, start, width, total):
    lo, hi = start - 128, start + width + 128
    if lo < 0:
        return jnp.concatenate([load(total + lo, total), load(0, hi)], axis=1)
    if hi > total:
        return jnp.concatenate([load(lo, total), load(0, hi - total)], axis=1)
    return load(lo, hi)


def west_east(load, start, width, total):
    wide = widened(load, start, width, total)
    span = width + 256
    west = pltpu.roll(wide, 1, 1)[:, 128:-128]
    east = pltpu.roll(wide, span - 1, 1)[:, 128:-128]
    return west, east


def south_north(rows):
    count = rows.shape[0]
    return pltpu.roll(rows, 1, 0), pltpu.roll(rows, count - 1, 0)


def kernel(
    R, F, seeds, dev, vel, frc, out_d, out_u,
    D, NZ, ST, SES, SER, ES, ER, U48, UU, RH, FP, CA, CB, TT, COEF, SPR,
    in_sem, out_sem, ses_s, ses_r, u_s, u_r, es_s, es_r,
    in_s, a_r, b_r, t_s, rh_s, rh_r, sp_s, sp_r,
):
    nf, NY = dev.shape[0], dev.shape[3]
    r = lax.axis_index("rows")
    f = lax.axis_index("fields")
    south = {"rows": lax.rem(r + R - 1, R)}
    north = {"rows": lax.rem(r + 1, R)}
    half = F // 2
    is_low = f < half
    inward = {"fields": jnp.where(is_low, f + 1, f - 1)}
    outward_index = jnp.where(is_low, f - 1, f + 1)
    not_end = jnp.logical_and(f > 0, f < F - 1)
    is_mid = jnp.logical_or(f == half - 1, f == half)
    outward = {"fields": jnp.clip(outward_index, 0, F - 1)}
    CW = NY // K
    W = 512
    NC = NY // W

    def remote(src, dst, s, q, device):
        return pltpu.make_async_remote_copy(
            src_ref=src, dst_ref=dst, send_sem=s, recv_sem=q, device_id=device, device_id_type=MESH
        )

    loads = [
        pltpu.make_async_copy(
            dev.at[:, :, :, pl.ds(c * W, W)], D.at[0, :, :, :, pl.ds(c * W, W)], in_sem.at[c]
        )
        for c in range(NC)
    ]
    for one in loads:
        one.start()

    barrier = pltpu.get_barrier_semaphore()
    for p in range(1, R):
        pl.semaphore_signal(barrier, inc=1, device_id={"rows": lax.rem(r + p, R)}, device_id_type=MESH)
    pl.semaphore_signal(barrier, inc=1, device_id=inward, device_id_type=MESH)

    @pl.when(not_end)
    def _():
        pl.semaphore_signal(barrier, inc=1, device_id=outward, device_id_type=MESH)

    def ses_copy(step, side):
        return remote(SES.at[step, side], SER.at[step, 1 - side], ses_s.at[step, side],
                      ses_r.at[step, 1 - side], south if side == 0 else north)

    def es_copy(step, side):
        return remote(ES.at[step, side], ER.at[step, 1 - side], es_s.at[step, side],
                      es_r.at[step, 1 - side], south if side == 0 else north)

    def u_copy(step, side):
        src = U48.at[step, :, pl.ds(16, 16)]
        dst = U48.at[step, :, pl.ds(32 if side == 0 else 0, 16)]
        return remote(src, dst, u_s.at[step, side], u_r.at[step, 1 - side], south if side == 0 else north)

    def cols(c):
        return pl.ds(c * CW, CW)

    def in_copy(step, c):
        return remote(FP.at[step, :, :, cols(c)], CA.at[step, :, :, cols(c)], in_s.at[step, c],
                      a_r.at[step, c], inward)

    def mid_copy(step, c):
        return remote(FP.at[step, :, :, cols(c)], CB.at[step, :, :, cols(c)], in_s.at[step, c],
                      b_r.at[step, c], inward)

    def total_copy(step, c):
        return remote(TT.at[step, :, :, cols(c)], CB.at[step, :, :, cols(c)], t_s.at[step, c],
                      b_r.at[step, c], outward)

    def rh_copy(step, side, c):
        src = RH.at[step, :, pl.ds(8 if side == 0 else 16, 8), cols(c)]
        dst = RH.at[step, :, pl.ds(24 if side == 0 else 0, 8), cols(c)]
        return remote(src, dst, rh_s.at[step, side, c], rh_r.at[step, 1 - side, c],
                      south if side == 0 else north)

    def sp_copy(step, p):
        return remote(SPR.at[step, 0], SPR.at[step, p], sp_s.at[step, p], sp_r.at[step, p],
                      {"rows": lax.rem(r + p, R)})

    def stress(step):
        for c in range(NC):
            if step == 0:
                loads[c].wait()
            at = slice(c * W, c * W + W)

            def add(i, acc):
                tensor = [D[step, i, m, :, at] for m in range(3)]
                for m in range(3):
                    ES[step, 0, pl.ds(3 * i + m, 1), at] = tensor[m][0:1]
                    ES[step, 1, pl.ds(3 * i + m, 1), at] = tensor[m][15:16]
                spring = (1.0 + 2.0 / LMAX2) + (tensor[0] + tensor[2]) * (1.0 / LMAX2)
                return tuple(acc[m] + spring * tensor[m] for m in range(3))

            zero = jnp.zeros((16, W), jnp.float32)
            acc = lax.fori_loop(0, nf, add, (zero, zero, zero))
            acc = [one * (G_COEF / FIELDS) for one in acc]
            for m in range(3):
                ST[m, :, at] = acc[m]
            for m in (1, 2):
                row = (m - 1) * NC + c
                SES[step, 0, row:row + 1, :] = acc[m][0:1]
                SES[step, 1, row:row + 1, :] = acc[m][15:16]

    row16 = lax.broadcasted_iota(jnp.int32, (16, W), 0)

    def with_edges(rows, low, high):
        down, up = south_north(rows)
        return jnp.where(row16 == 0, low, down), jnp.where(row16 == 15, high, up)

    def force(step, c):
        at = slice(c * W, c * W + W)
        for comp in range(2):
            west, east = west_east(lambda lo, hi: ST[comp, :, lo:hi], c * W, W, NY)
            row = comp * NC + c
            down, up = with_edges(ST[comp + 1, :, at], SER[step, 0, row:row + 1, :], SER[step, 1, row:row + 1, :])
            FP[step, comp, :, at] = ((east - west) + (up - down)) * 0.5

    iota_cells = lax.broadcasted_iota(jnp.int32, (16, W), 0) * NY + lax.broadcasted_iota(jnp.int32, (16, W), 1)

    def noise(step, lo, hi):
        if hi <= lo:
            return

        def one(i, _):
            base = seeds[i] * jnp.int32(2654435) + r * jnp.int32(16 * NY)
            for c in range(NC):
                for m in range(3):
                    h = iota_cells + (base + jnp.int32((3 * step + m) * 97531 + c * W))
                    h = jnp.bitwise_xor(h, lax.shift_right_logical(h, jnp.full_like(h, 16)))
                    h = h * jnp.int32(73244475)
                    h = jnp.bitwise_xor(h, lax.shift_right_logical(h, jnp.full_like(h, 16)))
                    h = h * jnp.int32(73244475)
                    h = jnp.bitwise_xor(h, lax.shift_right_logical(h, jnp.full_like(h, 16)))
                    h = jnp.bitwise_and(h, jnp.int32(65535)).astype(jnp.float32)
                    NZ[i, m, :, c * W:c * W + W] = (h - 32767.5) * (SIGMA / 18918.6)
            return 0

        lax.fori_loop(lo, hi, one, 0)

    def chain(step):
        for i in range(K + LAG):
            if i < K:
                @pl.when(not_end)
                def _():
                    in_copy(step, i).wait_recv()
                    at = slice(i * CW, i * CW + CW)
                    FP[step, :, :, at] = FP[step, :, :, at] + CA[step, :, :, at]

                @pl.when(is_mid)
                def _():
                    mid_copy(step, i).start()

                @pl.when(jnp.logical_not(is_mid))
                def _():
                    in_copy(step, i).start()

                noise(step, i * nf // 16, (i + 1) * nf // 16)
            if i >= LAG:
                j = i - LAG
                at = slice(j * CW, j * CW + CW)
                mid_copy(step, j).wait_recv()
                got = CB[step, :, :, at]
                total = jnp.where(is_mid, FP[step, :, :, at] + got, got)
                TT[step, :, :, at] = total

                @pl.when(not_end)
                def _():
                    total_copy(step, j).start()

                RH[step, :, 8:24, at] = frc[:, :, at] + total
                rh_copy(step, 0, j).start()
                rh_copy(step, 1, j).start()

    factor = 1.0 / (ALPHA + 4.0)

    def solve(step):
        for comp in range(2):
            for c in range(NC):
                at = slice(c * W, c * W + W)
                west, east = west_east(lambda lo, hi: U48[step, comp, 8:40, lo:hi], c * W, W, NY)
                down, up = south_north(U48[step, comp, :, at])
                beside = (up[8:40] + down[8:40]) + (east + west)
                UU[1, comp, :, at] = (RH[step, comp, :, at] + beside) * factor

        def sweep(k, _):
            src, dst = lax.rem(k + 1, 2), lax.rem(k, 2)
            for comp in range(2):
                for c in range(NC):
                    at = slice(c * W, c * W + W)
                    west, east = west_east(lambda lo, hi: UU[src, comp, :, lo:hi], c * W, W, NY)
                    down, up = south_north(UU[src, comp, :, at])
                    UU[dst, comp, :, at] = (RH[step, comp, :, at] + ((up + down) + (east + west))) * factor
            return 0

        lax.fori_loop(2, SWEEPS + 1, sweep, 0)

    def local_speed(step):
        top = None
        for c in range(NC):
            at = slice(c * W, c * W + W)
            one = jnp.abs(UU[0, 0, 8:24, at]) + jnp.abs(UU[0, 1, 8:24, at])
            one = jnp.maximum(one[0:8], one[8:16])
            for q in range(W // 128):
                part = one[:, q * 128:q * 128 + 128]
                top = part if top is None else jnp.maximum(top, part)
        SPR[step, 0] = top
        for p in range(1, R):
            sp_copy(step, p).start()

    def coefficients(step):
        top = SPR[step, 0]
        for p in range(1, R):
            sp_copy(step, p).wait_recv()
            top = jnp.maximum(top, SPR[step, p])
        top = jnp.max(jnp.max(top, axis=1, keepdims=True), axis=0, keepdims=True)
        dt = DT / (1.0 + top)
        root = jnp.sqrt(dt)
        for c in range(NC):
            at = slice(c * W, c * W + W)
            grads = []
            for comp in range(2):
                west, east = west_east(lambda lo, hi: UU[0, comp, 8:24, lo:hi], c * W, W, NY)
                down, up = south_north(UU[0, comp, :, at])
                grads.append((east - west) * 0.5)
                grads.append((up[8:24] - down[8:24]) * 0.5)
            lxx, lxy, lyx, lyy = [one * dt for one in grads]
            ux, uy = UU[0, 0, 8:24, at] * dt, UU[0, 1, 8:24, at] * dt
            centre = 1.0 - (jnp.abs(ux) + jnp.abs(uy)) - dt * ((1.0 + 2.0 / LMAX2) / LAMBDA)
            values = (
                jnp.maximum(ux, 0.0), -jnp.minimum(ux, 0.0), jnp.maximum(uy, 0.0), -jnp.minimum(uy, 0.0),
                centre + 2.0 * lxx, centre + (lxx + lyy), centre + 2.0 * lyy,
                lxy, lyx, lxx + lxx, lxy + lyx, lyy + lyy,
            )
            for k, one in enumerate(values):
                COEF[k, :, at] = one
        return dt, root

    AW = 256
    row_a = lax.broadcasted_iota(jnp.int32, (16, AW), 0)

    def store_out(i):
        return pltpu.make_async_copy(D.at[0, i], out_d.at[i], out_sem.at[i])

    def advance(step, dt, root):
        pull = jnp.broadcast_to(dt * (1.0 / (LMAX2 * LAMBDA)), (16, AW))
        loud = jnp.broadcast_to(root, (16, AW))

        def one(i, _):
            for c in range(NY // AW):
                at = slice(c * AW, c * AW + AW)
                a, b, d = [D[step, i, m, :, at] for m in range(3)]
                q = (a + d) * pull
                lxy, lyx = COEF[7, :, at], COEF[8, :, at]
                xb, yb = lxy * b, lyx * b
                cross = (xb + xb, lxy * d + lyx * a, yb + yb)
                for m, x in enumerate((a, b, d)):
                    west, east = west_east(lambda lo, hi: D[step, i, m, :, lo:hi], c * AW, AW, NY)
                    down, up = south_north(x)
                    down = jnp.where(row_a == 0, ER[step, 0, pl.ds(3 * i + m, 1), at], down)
                    up = jnp.where(row_a == 15, ER[step, 1, pl.ds(3 * i + m, 1), at], up)
                    fresh = (COEF[4 + m, :, at] - q) * x + cross[m]
                    fresh = fresh + (COEF[0, :, at] * west + COEF[1, :, at] * east)
                    fresh = fresh + (COEF[2, :, at] * down + COEF[3, :, at] * up)
                    D[1 - step, i, m, :, at] = fresh + (COEF[9 + m, :, at] + loud * NZ[i, m, :, at])
            if step == STEPS - 1:
                store_out(i).start()
            return 0

        lax.fori_loop(0, nf, one, 0)

    U48[0, :, 16:32] = vel[...]
    for step in range(STEPS):
        stress(step)
        if step == 0:
            pl.semaphore_wait(barrier, jnp.where(not_end, R + 1, R))
        for side in range(2):
            ses_copy(step, side).start()
        if step == 0:
            for side in range(2):
                u_copy(step, side).start()
        for side in range(2):
            es_copy(step, side).start()
        for side in range(2):
            ses_copy(step, side).wait_recv()
        for c in range(NC):
            force(step, c)
        chain(step)
        noise(step, nf // 2, 3 * nf // 4)
        for side in range(2):
            u_copy(step, side).wait_recv()
            for c in range(K):
                rh_copy(step, side, c).wait_recv()
        solve(step)
        local_speed(step)
        if step < STEPS - 1:
            U48[step + 1, :, 16:32] = UU[0, :, 8:24]
            for side in range(2):
                u_copy(step + 1, side).start()
        else:
            out_u[...] = UU[0, :, 8:24]
        noise(step, 3 * nf // 4, nf)
        dt, root = coefficients(step)
        for side in range(2):
            es_copy(step, side).wait_recv()
        advance(step, dt, root)

    for step in range(STEPS):
        for side in range(2):
            ses_copy(step, side).wait_send()
            u_copy(step, side).wait_send()
            es_copy(step, side).wait_send()
        for c in range(K):
            in_copy(step, c).wait_send()
            rh_copy(step, 0, c).wait_send()
            rh_copy(step, 1, c).wait_send()
        for p in range(1, R):
            sp_copy(step, p).wait_send()

        @pl.when(not_end)
        def _():
            for c in range(K):
                total_copy(step, c).wait_send()

    def finish(i, _):
        store_out(i).wait()
        return 0

    lax.fori_loop(0, nf, finish, 0)


def body(R, F, deviation, seeds, velocity, forcing):
    nf, _, rows, NY = deviation.shape
    f32 = jnp.float32
    S = STEPS
    dma = pltpu.SemaphoreType.DMA
    vmem = lambda *shape: pltpu.VMEM(shape, f32)
    return pl.pallas_call(
        functools.partial(kernel, R, F),
        out_shape=(
            jax.ShapeDtypeStruct(deviation.shape, f32),
            jax.ShapeDtypeStruct(velocity.shape, f32),
        ),
        in_specs=[
            pl.BlockSpec(memory_space=pltpu.SMEM),
            pl.BlockSpec(memory_space=pl.ANY),
            pl.BlockSpec(memory_space=pltpu.VMEM),
            pl.BlockSpec(memory_space=pltpu.VMEM),
        ],
        out_specs=(pl.BlockSpec(memory_space=pl.ANY), pl.BlockSpec(memory_space=pltpu.VMEM)),
        scratch_shapes=[
            vmem(2, nf, 3, rows, NY), vmem(nf, 3, rows, NY), vmem(3, rows, NY),
            vmem(S, 2, 8, 512), vmem(S, 2, 8, 512),
            vmem(S, 2, nf * 3, NY), vmem(S, 2, nf * 3, NY),
            vmem(S, 2, 48, NY), vmem(2, 2, 32, NY), vmem(S, 2, 32, NY),
            vmem(S, 2, rows, NY), vmem(S, 2, rows, NY), vmem(S, 2, rows, NY), vmem(S, 2, rows, NY),
            vmem(12, rows, NY), vmem(S, R, 8, 128),
            dma((4,)), dma((nf,)),
            dma((S, 2)), dma((S, 2)), dma((S, 2)), dma((S, 2)), dma((S, 2)), dma((S, 2)),
            dma((S, K)), dma((S, K)), dma((S, K)), dma((S, K)),
            dma((S, 2, K)), dma((S, 2, K)), dma((S, R)), dma((S, R)),
        ],
        compiler_params=pltpu.CompilerParams(
            collective_id=0, has_side_effects=True, vmem_limit_bytes=52 * 1024 * 1024
        ),
    )(seeds, deviation, velocity, forcing)


def solution(mesh):
    return jax.shard_map(
        functools.partial(body, mesh.shape["rows"], mesh.shape["fields"]),
        mesh=mesh,
        in_specs=(
            P("fields", None, "rows", None),
            P("fields"),
            P(None, "rows", None),
            P(None, "rows", None),
        ),
        out_specs=(P("fields", None, "rows", None), P(None, "rows", None)),
        check_vma=False,
    )
```

```python
import functools

import jax
import jax.numpy as jnp
from jax import lax
from jax.experimental import pallas as pl
from jax.experimental.pallas import tpu as pltpu
from jax.sharding import PartitionSpec as P

FIELDS = 64
SWEEPS = 8
STEPS = 2

G_COEF = 4.0
ALPHA = 0.05
LMAX2 = 20.0
LAMBDA = 1.0
DT = 0.2
SIGMA = 1.0

K = 8
LAG = 2
MESH = pl.DeviceIdType.MESH


def widened(load, start, width, total):
    lo, hi = start - 128, start + width + 128
    if lo < 0:
        return jnp.concatenate([load(total + lo, total), load(0, hi)], axis=1)
    if hi > total:
        return jnp.concatenate([load(lo, total), load(0, hi - total)], axis=1)
    return load(lo, hi)


def west_east(load, start, width, total):
    wide = widened(load, start, width, total)
    span = width + 256
    west = pltpu.roll(wide, 1, 1)[:, 128:-128]
    east = pltpu.roll(wide, span - 1, 1)[:, 128:-128]
    return west, east


def tiles_with_sides(load, count):
    before = pltpu.roll(load(count - 1), 1, 1)
    here = load(0)
    here_w, here_e = pltpu.roll(here, 1, 1), pltpu.roll(here, 127, 1)
    lane = lax.broadcasted_iota(jnp.int32, here.shape, 1)
    first, last = lane == 0, lane == 127
    for j in range(count):
        after = load((j + 1) % count)
        after_w, after_e = pltpu.roll(after, 1, 1), pltpu.roll(after, 127, 1)
        yield j, here, jnp.where(first, before, here_w), jnp.where(last, after_e, here_e)
        before, here, here_w, here_e = here_w, after, after_w, after_e


def south_north(rows):
    count = rows.shape[0]
    return pltpu.roll(rows, 1, 0), pltpu.roll(rows, count - 1, 0)


def kernel(
    R, F, seeds_in, dev, vel, frc, out_d, out_u,
    D, NZ, ST, SES, SER, ES, ER, U32, XS, XR, UU, RH, FR, SD, FP, CA, CB, TT, COEF, SPR,
    in_sem, arg_sem, out_sem, ses_s, ses_r, u_s, u_r, x_s, x_r, es_s, es_r,
    in_s, a_r, b_r, t_s, rh_s, rh_r, sp_s, sp_r,
):
    nf, NY = dev.shape[0], dev.shape[3]
    r = lax.axis_index("rows")
    f = lax.axis_index("fields")
    south = {"rows": lax.rem(r + R - 1, R)}
    north = {"rows": lax.rem(r + 1, R)}
    half = F // 2
    is_low = f < half
    inward = {"fields": jnp.where(is_low, f + 1, f - 1)}
    outward_index = jnp.where(is_low, f - 1, f + 1)
    not_end = jnp.logical_and(f > 0, f < F - 1)
    is_mid = jnp.logical_or(f == half - 1, f == half)
    outward = {"fields": jnp.clip(outward_index, 0, F - 1)}
    CW = NY // K
    W = 512
    NC = NY // W

    def remote(src, dst, s, q, device):
        return pltpu.make_async_remote_copy(
            src_ref=src, dst_ref=dst, send_sem=s, recv_sem=q, device_id=device, device_id_type=MESH
        )

    loads = [
        pltpu.make_async_copy(
            dev.at[:, :, :, pl.ds(c * W, W)], D.at[0, :, :, :, pl.ds(c * W, W)], in_sem.at[c]
        )
        for c in range(NC)
    ]
    for one in loads:
        one.start()

    seed_load = pltpu.make_async_copy(seeds_in, SD, arg_sem.at[0])
    vel_load = pltpu.make_async_copy(vel, U32.at[0, :, pl.ds(8, 16)], arg_sem.at[1])
    frc_load = pltpu.make_async_copy(frc, FR, arg_sem.at[2])
    vel_load.start()
    frc_load.start()
    seed_load.start()
    barrier = pltpu.get_barrier_semaphore()
    for p in range(1, R):
        pl.semaphore_signal(barrier, inc=1, device_id={"rows": lax.rem(r + p, R)}, device_id_type=MESH)
    pl.semaphore_signal(barrier, inc=1, device_id=inward, device_id_type=MESH)

    @pl.when(not_end)
    def _():
        pl.semaphore_signal(barrier, inc=1, device_id=outward, device_id_type=MESH)

    def ses_copy(step, side):
        return remote(SES.at[step, side], SER.at[step, 1 - side], ses_s.at[step, side],
                      ses_r.at[step, 1 - side], south if side == 0 else north)

    def es_copy(step, side):
        return remote(ES.at[step, side], ER.at[step, 1 - side], es_s.at[step, side],
                      es_r.at[step, 1 - side], south if side == 0 else north)

    def u_copy(step, side):
        src = U32.at[step, :, pl.ds(8 if side == 0 else 16, 8)]
        dst = U32.at[step, :, pl.ds(24 if side == 0 else 0, 8)]
        return remote(src, dst, u_s.at[step, side], u_r.at[step, 1 - side], south if side == 0 else north)

    def x_copy(step, side):
        return remote(XS.at[step, side], XR.at[step, 1 - side], x_s.at[step, side],
                      x_r.at[step, 1 - side], south if side == 0 else north)

    def send_velocity(step):
        for comp in range(2):
            for c in range(NC):
                row = comp * NC + c
                at = slice(c * W, c * W + W)
                XS[step, 0, row:row + 1, :] = U32[step, comp, 16:24, at][0:1]
                XS[step, 1, row:row + 1, :] = U32[step, comp, 8:16, at][7:8]
        for side in range(2):
            u_copy(step, side).start()
            x_copy(step, side).start()

    def cols(c):
        return pl.ds(c * CW, CW)

    def in_copy(step, c):
        return remote(FP.at[step, :, :, cols(c)], CA.at[step, :, :, cols(c)], in_s.at[step, c],
                      a_r.at[step, c], inward)

    def mid_copy(step, c):
        return remote(FP.at[step, :, :, cols(c)], CB.at[step, :, :, cols(c)], in_s.at[step, c],
                      b_r.at[step, c], inward)

    def total_copy(step, c):
        return remote(TT.at[step, :, :, cols(c)], CB.at[step, :, :, cols(c)], t_s.at[step, c],
                      b_r.at[step, c], outward)

    def rh_copy(step, side, c):
        src = RH.at[step, :, pl.ds(8 if side == 0 else 16, 8), cols(c)]
        dst = RH.at[step, :, pl.ds(24 if side == 0 else 0, 8), cols(c)]
        return remote(src, dst, rh_s.at[step, side, c], rh_r.at[step, 1 - side, c],
                      south if side == 0 else north)

    def sp_copy(step, p):
        return remote(SPR.at[step, 0], SPR.at[step, p], sp_s.at[step, p], sp_r.at[step, p],
                      {"rows": lax.rem(r + p, R)})

    def stress(step):
        for c in range(NC):
            if step == 0:
                loads[c].wait()
            at = slice(c * W, c * W + W)

            def add(i, acc):
                tensor = [D[step, i, m, :, at] for m in range(3)]
                for m in range(3):
                    ES[step, 0, pl.ds(3 * i + m, 1), at] = tensor[m][0:1]
                    ES[step, 1, pl.ds(3 * i + m, 1), at] = tensor[m][15:16]
                spring = (1.0 + 2.0 / LMAX2) + (tensor[0] + tensor[2]) * (1.0 / LMAX2)
                return tuple(acc[m] + spring * tensor[m] for m in range(3))

            zero = jnp.zeros((16, W), jnp.float32)
            acc = lax.fori_loop(0, nf, add, (zero, zero, zero))
            acc = [one * (G_COEF / FIELDS) for one in acc]
            for m in range(3):
                ST[m, :, at] = acc[m]
            for m in (1, 2):
                row = (m - 1) * NC + c
                SES[step, 0, row:row + 1, :] = acc[m][0:1]
                SES[step, 1, row:row + 1, :] = acc[m][15:16]

    row16 = lax.broadcasted_iota(jnp.int32, (16, W), 0)

    def with_edges(rows, low, high):
        down, up = south_north(rows)
        return jnp.where(row16 == 0, low, down), jnp.where(row16 == 15, high, up)

    def force(step, c):
        at = slice(c * W, c * W + W)
        for comp in range(2):
            west, east = west_east(lambda lo, hi: ST[comp, :, lo:hi], c * W, W, NY)
            row = comp * NC + c
            down, up = with_edges(ST[comp + 1, :, at], SER[step, 0, row:row + 1, :], SER[step, 1, row:row + 1, :])
            FP[step, comp, :, at] = ((east - west) + (up - down)) * 0.5

    iota_cells = lax.broadcasted_iota(jnp.int32, (16, W), 0) * NY + lax.broadcasted_iota(jnp.int32, (16, W), 1)

    def noise(step, lo, hi):
        if hi <= lo:
            return

        def one(i, _):
            base = SD[i] * jnp.int32(2654435) + r * jnp.int32(16 * NY)
            for c in range(NC):
                for m in range(3):
                    h = iota_cells + (base + jnp.int32((3 * step + m) * 97531 + c * W))
                    h = jnp.bitwise_xor(h, lax.shift_right_logical(h, jnp.full_like(h, 16)))
                    h = h * jnp.int32(73244475)
                    h = jnp.bitwise_xor(h, lax.shift_right_logical(h, jnp.full_like(h, 16)))
                    h = h * jnp.int32(73244475)
                    h = jnp.bitwise_xor(h, lax.shift_right_logical(h, jnp.full_like(h, 16)))
                    h = jnp.bitwise_and(h, jnp.int32(65535)).astype(jnp.float32)
                    NZ[i, m, :, c * W:c * W + W] = h
            return 0

        lax.fori_loop(lo, hi, one, 0)

    def chain(step):
        for i in range(K + LAG):
            if i < K:
                @pl.when(not_end)
                def _():
                    in_copy(step, i).wait_recv()
                    at = slice(i * CW, i * CW + CW)
                    FP[step, :, :, at] = FP[step, :, :, at] + CA[step, :, :, at]

                @pl.when(is_mid)
                def _():
                    mid_copy(step, i).start()

                @pl.when(jnp.logical_not(is_mid))
                def _():
                    in_copy(step, i).start()

                noise(step, i * nf // 16, (i + 1) * nf // 16)
            if i >= LAG:
                j = i - LAG
                at = slice(j * CW, j * CW + CW)
                mid_copy(step, j).wait_recv()
                got = CB[step, :, :, at]
                total = jnp.where(is_mid, FP[step, :, :, at] + got, got)
                TT[step, :, :, at] = total

                @pl.when(not_end)
                def _():
                    total_copy(step, j).start()

                RH[step, :, 8:24, at] = FR[:, :, at] + total
                rh_copy(step, 0, j).start()
                rh_copy(step, 1, j).start()

    factor = 1.0 / (ALPHA + 4.0)

    NT = NY // 128

    def solve(step):
        row32 = lax.broadcasted_iota(jnp.int32, (32, 128), 0)
        for comp in range(2):
            for j, here, west, east in tiles_with_sides(
                lambda j: U32[step, comp, :, j * 128:j * 128 + 128], NT
            ):
                at = slice(j * 128, j * 128 + 128)
                row, part = comp * NC + j * 128 // W, j * 128 % W
                down, up = south_north(here)
                down = jnp.where(row32 == 0, XR[step, 0, row:row + 1, part:part + 128], down)
                up = jnp.where(row32 == 31, XR[step, 1, row:row + 1, part:part + 128], up)
                UU[1, comp, :, at] = (RH[step, comp, :, at] + ((up + down) + (east + west))) * factor

        def sweep(k, _):
            src, dst = lax.rem(k + 1, 2), lax.rem(k, 2)
            for comp in range(2):
                for j, here, west, east in tiles_with_sides(
                    lambda j: UU[src, comp, :, j * 128:j * 128 + 128], NT
                ):
                    at = slice(j * 128, j * 128 + 128)
                    down, up = south_north(here)
                    UU[dst, comp, :, at] = (RH[step, comp, :, at] + ((up + down) + (east + west))) * factor
            return 0

        lax.fori_loop(2, SWEEPS + 1, sweep, 0)

    def local_speed(step):
        top = None
        for c in range(NC):
            at = slice(c * W, c * W + W)
            one = jnp.abs(UU[0, 0, 8:24, at]) + jnp.abs(UU[0, 1, 8:24, at])
            one = jnp.maximum(one[0:8], one[8:16])
            for q in range(W // 128):
                part = one[:, q * 128:q * 128 + 128]
                top = part if top is None else jnp.maximum(top, part)
        SPR[step, 0] = top
        for p in range(1, R):
            sp_copy(step, p).start()

    def coefficients(step):
        top = SPR[step, 0]
        for p in range(1, R):
            sp_copy(step, p).wait_recv()
            top = jnp.maximum(top, SPR[step, p])
        top = jnp.max(jnp.max(top, axis=1, keepdims=True), axis=0, keepdims=True)
        dt = DT / (1.0 + top)
        loud = jnp.sqrt(dt) * (SIGMA / 18918.6)
        shift = loud * 32767.5
        for c in range(NC):
            at = slice(c * W, c * W + W)
            grads = []
            for comp in range(2):
                west, east = west_east(lambda lo, hi: UU[0, comp, 8:24, lo:hi], c * W, W, NY)
                down, up = south_north(UU[0, comp, :, at])
                grads.append((east - west) * 0.5)
                grads.append((up[8:24] - down[8:24]) * 0.5)
            lxx, lxy, lyx, lyy = [one * dt for one in grads]
            ux, uy = UU[0, 0, 8:24, at] * dt, UU[0, 1, 8:24, at] * dt
            centre = 1.0 - (jnp.abs(ux) + jnp.abs(uy)) - dt * ((1.0 + 2.0 / LMAX2) / LAMBDA)
            values = (
                jnp.maximum(ux, 0.0), -jnp.minimum(ux, 0.0), jnp.maximum(uy, 0.0), -jnp.minimum(uy, 0.0),
                centre + 2.0 * lxx, centre + (lxx + lyy), centre + 2.0 * lyy,
                lxy, lyx, (lxx + lxx) - shift, (lxy + lyx) - shift, (lyy + lyy) - shift,
            )
            for k, one in enumerate(values):
                COEF[k, :, at] = one
        return dt, loud

    row_a = lax.broadcasted_iota(jnp.int32, (16, 128), 0)

    def store_out(i):
        return pltpu.make_async_copy(D.at[0, i], out_d.at[i], out_sem.at[i])

    def advance(step, dt, loud):
        pull = jnp.broadcast_to(dt * (1.0 / (LMAX2 * LAMBDA)), (16, 128))
        loud = jnp.broadcast_to(loud, (16, 128))

        def one(i, _):
            def walk(m):
                return tiles_with_sides(lambda j: D[step, i, m, :, j * 128:j * 128 + 128], NT)

            for both in zip(walk(0), walk(1), walk(2)):
                j = both[0][0]
                at = slice(j * 128, j * 128 + 128)
                if j % 2 == 0:
                    pair = slice(j * 128, j * 128 + 256)
                    rims = [
                        [ER[step, side, pl.ds(3 * i + m, 1), pair] for m in range(3)] for side in range(2)
                    ]
                part = slice(j % 2 * 128, j % 2 * 128 + 128)
                a, b, d = [one[1] for one in both]
                q = (a + d) * pull
                xb, yb = COEF[7, :, at] * b, COEF[8, :, at] * b
                cross = (xb + xb, COEF[7, :, at] * d + COEF[8, :, at] * a, yb + yb)
                cw, ce, cs, cn = [COEF[k, :, at] for k in range(4)]
                for m, (_, x, west, east) in enumerate(both):
                    down, up = south_north(x)
                    down = jnp.where(row_a == 0, rims[0][m][:, part], down)
                    up = jnp.where(row_a == 15, rims[1][m][:, part], up)
                    fresh = (COEF[4 + m, :, at] - q) * x + cross[m]
                    fresh = fresh + (cw * west + ce * east)
                    fresh = fresh + (cs * down + cn * up)
                    D[1 - step, i, m, :, at] = fresh + (COEF[9 + m, :, at] + loud * NZ[i, m, :, at])
            if step == STEPS - 1:
                store_out(i).start()
            return 0

        lax.fori_loop(0, nf, one, 0)

    for step in range(STEPS):
        stress(step)
        if step == 0:
            pl.semaphore_wait(barrier, jnp.where(not_end, R + 1, R))
        for side in range(2):
            ses_copy(step, side).start()
        if step == 0:
            vel_load.wait()
            send_velocity(step)
            frc_load.wait()
            seed_load.wait()
        for side in range(2):
            es_copy(step, side).start()
        for side in range(2):
            ses_copy(step, side).wait_recv()
        for c in range(NC):
            force(step, c)
        chain(step)
        noise(step, nf // 2, 3 * nf // 4)
        for side in range(2):
            u_copy(step, side).wait_recv()
            x_copy(step, side).wait_recv()
            for c in range(K):
                rh_copy(step, side, c).wait_recv()
        solve(step)
        local_speed(step)
        if step < STEPS - 1:
            U32[step + 1, :, 8:24] = UU[0, :, 8:24]
            send_velocity(step + 1)
        else:
            out_u[...] = UU[0, :, 8:24]
        noise(step, 3 * nf // 4, nf)
        dt, loud = coefficients(step)
        for side in range(2):
            es_copy(step, side).wait_recv()
        advance(step, dt, loud)

    for step in range(STEPS):
        for side in range(2):
            ses_copy(step, side).wait_send()
            u_copy(step, side).wait_send()
            x_copy(step, side).wait_send()
            es_copy(step, side).wait_send()
        for c in range(K):
            in_copy(step, c).wait_send()
            rh_copy(step, 0, c).wait_send()
            rh_copy(step, 1, c).wait_send()
        for p in range(1, R):
            sp_copy(step, p).wait_send()

        @pl.when(not_end)
        def _():
            for c in range(K):
                total_copy(step, c).wait_send()

    def finish(i, _):
        store_out(i).wait()
        return 0

    lax.fori_loop(0, nf, finish, 0)


def body(R, F, deviation, seeds, velocity, forcing):
    nf, _, rows, NY = deviation.shape
    f32 = jnp.float32
    S = STEPS
    dma = pltpu.SemaphoreType.DMA
    vmem = lambda *shape: pltpu.VMEM(shape, f32)
    return pl.pallas_call(
        functools.partial(kernel, R, F),
        out_shape=(
            jax.ShapeDtypeStruct(deviation.shape, f32),
            jax.ShapeDtypeStruct(velocity.shape, f32),
        ),
        in_specs=[
            pl.BlockSpec(memory_space=pl.ANY),
            pl.BlockSpec(memory_space=pl.ANY),
            pl.BlockSpec(memory_space=pl.ANY),
            pl.BlockSpec(memory_space=pl.ANY),
        ],
        out_specs=(pl.BlockSpec(memory_space=pl.ANY), pl.BlockSpec(memory_space=pltpu.VMEM)),
        scratch_shapes=[
            vmem(2, nf, 3, rows, NY), vmem(nf, 3, rows, NY), vmem(3, rows, NY),
            vmem(S, 2, 8, 512), vmem(S, 2, 8, 512),
            vmem(S, 2, nf * 3, NY), vmem(S, 2, nf * 3, NY),
            vmem(S, 2, 32, NY), vmem(S, 2, 8, 512), vmem(S, 2, 8, 512),
            vmem(2, 2, 32, NY), vmem(S, 2, 32, NY), vmem(2, rows, NY), pltpu.SMEM((nf,), jnp.int32),
            vmem(S, 2, rows, NY), vmem(S, 2, rows, NY), vmem(S, 2, rows, NY), vmem(S, 2, rows, NY),
            vmem(12, rows, NY), vmem(S, R, 8, 128),
            dma((4,)), dma((3,)), dma((nf,)),
            *[dma((S, 2))] * 8,
            dma((S, K)), dma((S, K)), dma((S, K)), dma((S, K)),
            dma((S, 2, K)), dma((S, 2, K)), dma((S, R)), dma((S, R)),
        ],
        compiler_params=pltpu.CompilerParams(
            collective_id=0, has_side_effects=True, vmem_limit_bytes=63 * 1024 * 1024
        ),
    )(seeds, deviation, velocity, forcing)


def solution(mesh):
    return jax.shard_map(
        functools.partial(body, mesh.shape["rows"], mesh.shape["fields"]),
        mesh=mesh,
        in_specs=(
            P("fields", None, "rows", None),
            P("fields"),
            P(None, "rows", None),
            P(None, "rows", None),
        ),
        out_specs=(P("fields", None, "rows", None), P(None, "rows", None)),
        check_vma=False,
    )
```

```python
import functools

import jax
import jax.numpy as jnp
from jax import lax
from jax.experimental import pallas as pl
from jax.experimental.pallas import tpu as pltpu
from jax.sharding import PartitionSpec as P

FIELDS = 64
SWEEPS = 8
STEPS = 2

G_COEF = 4.0
ALPHA = 0.05
LMAX2 = 20.0
LAMBDA = 1.0
DT = 0.2
SIGMA = 1.0

K = 8
LAG = 3
MESH = pl.DeviceIdType.MESH


def widened(load, start, width, total):
    lo, hi = start - 128, start + width + 128
    if lo < 0:
        return jnp.concatenate([load(total + lo, total), load(0, hi)], axis=1)
    if hi > total:
        return jnp.concatenate([load(lo, total), load(0, hi - total)], axis=1)
    return load(lo, hi)


def west_east(load, start, width, total):
    wide = widened(load, start, width, total)
    span = width + 256
    west = pltpu.roll(wide, 1, 1)[:, 128:-128]
    east = pltpu.roll(wide, span - 1, 1)[:, 128:-128]
    return west, east


def tiles_with_sides(load, count):
    before = pltpu.roll(load(count - 1), 1, 1)
    here = load(0)
    here_w, here_e = pltpu.roll(here, 1, 1), pltpu.roll(here, 127, 1)
    lane = lax.broadcasted_iota(jnp.int32, here.shape, 1)
    first, last = lane == 0, lane == 127
    for j in range(count):
        after = load((j + 1) % count)
        after_w, after_e = pltpu.roll(after, 1, 1), pltpu.roll(after, 127, 1)
        yield j, here, jnp.where(first, before, here_w), jnp.where(last, after_e, here_e)
        before, here, here_w, here_e = here_w, after, after_w, after_e


def south_north(rows):
    count = rows.shape[0]
    return pltpu.roll(rows, 1, 0), pltpu.roll(rows, count - 1, 0)


def kernel(
    R, F, seeds_in, dev, vel, frc, out_d, out_u,
    D, NZ, ST, SES, SER, ES, ER, U32, XS, XR, UU, RH, FR, SD, FP, CA, CB, TT, COEF, SPR,
    in_sem, arg_sem, out_sem, ses_s, ses_r, u_s, u_r, x_s, x_r, es_s, es_r,
    in_s, a_r, b_r, t_s, rh_s, rh_r, sp_s, sp_r,
):
    nf, NY = dev.shape[0], dev.shape[3]
    r = lax.axis_index("rows")
    f = lax.axis_index("fields")
    south = {"rows": lax.rem(r + R - 1, R)}
    north = {"rows": lax.rem(r + 1, R)}
    half = F // 2
    is_low = f < half
    inward = {"fields": jnp.where(is_low, f + 1, f - 1)}
    outward_index = jnp.where(is_low, f - 1, f + 1)
    not_end = jnp.logical_and(f > 0, f < F - 1)
    is_mid = jnp.logical_or(f == half - 1, f == half)
    outward = {"fields": jnp.clip(outward_index, 0, F - 1)}
    CW = NY // K
    W = 512
    NC = NY // W

    def remote(src, dst, s, q, device):
        return pltpu.make_async_remote_copy(
            src_ref=src, dst_ref=dst, send_sem=s, recv_sem=q, device_id=device, device_id_type=MESH
        )

    loads = [
        pltpu.make_async_copy(
            dev.at[:, :, :, pl.ds(c * W, W)], D.at[0, :, :, :, pl.ds(c * W, W)], in_sem.at[c]
        )
        for c in range(NC)
    ]
    for one in loads:
        one.start()

    seed_load = pltpu.make_async_copy(seeds_in, SD, arg_sem.at[0])
    vel_load = pltpu.make_async_copy(vel, U32.at[0, :, pl.ds(8, 16)], arg_sem.at[1])
    frc_load = pltpu.make_async_copy(frc, FR, arg_sem.at[2])
    vel_load.start()
    frc_load.start()
    seed_load.start()
    barrier = pltpu.get_barrier_semaphore()
    for p in range(1, R):
        pl.semaphore_signal(barrier, inc=1, device_id={"rows": lax.rem(r + p, R)}, device_id_type=MESH)
    pl.semaphore_signal(barrier, inc=1, device_id=inward, device_id_type=MESH)

    @pl.when(not_end)
    def _():
        pl.semaphore_signal(barrier, inc=1, device_id=outward, device_id_type=MESH)

    def ses_copy(step, side):
        return remote(SES.at[step, side], SER.at[step, 1 - side], ses_s.at[step, side],
                      ses_r.at[step, 1 - side], south if side == 0 else north)

    def es_copy(step, side):
        return remote(ES.at[step, side], ER.at[step, 1 - side], es_s.at[step, side],
                      es_r.at[step, 1 - side], south if side == 0 else north)

    def u_copy(step, side):
        src = U32.at[step, :, pl.ds(8 if side == 0 else 16, 8)]
        dst = U32.at[step, :, pl.ds(24 if side == 0 else 0, 8)]
        return remote(src, dst, u_s.at[step, side], u_r.at[step, 1 - side], south if side == 0 else north)

    def x_copy(step, side):
        return remote(XS.at[step, side], XR.at[step, 1 - side], x_s.at[step, side],
                      x_r.at[step, 1 - side], south if side == 0 else north)

    def send_velocity(step):
        for comp in range(2):
            for c in range(NC):
                row = comp * NC + c
                at = slice(c * W, c * W + W)
                XS[step, 0, row:row + 1, :] = U32[step, comp, 16:24, at][0:1]
                XS[step, 1, row:row + 1, :] = U32[step, comp, 8:16, at][7:8]
        for side in range(2):
            u_copy(step, side).start()
            x_copy(step, side).start()

    def cols(c):
        return pl.ds(c * CW, CW)

    def in_copy(step, c):
        return remote(FP.at[step, :, :, cols(c)], CA.at[step, :, :, cols(c)], in_s.at[step, c],
                      a_r.at[step, c], inward)

    def mid_copy(step, c):
        return remote(FP.at[step, :, :, cols(c)], CB.at[step, :, :, cols(c)], in_s.at[step, c],
                      b_r.at[step, c], inward)

    def total_copy(step, c):
        return remote(TT.at[step, :, :, cols(c)], CB.at[step, :, :, cols(c)], t_s.at[step, c],
                      b_r.at[step, c], outward)

    def rh_copy(step, side, c):
        src = RH.at[step, :, pl.ds(8 if side == 0 else 16, 8), cols(c)]
        dst = RH.at[step, :, pl.ds(24 if side == 0 else 0, 8), cols(c)]
        return remote(src, dst, rh_s.at[step, side, c], rh_r.at[step, 1 - side, c],
                      south if side == 0 else north)

    def sp_copy(step, p):
        return remote(SPR.at[step, 0], SPR.at[step, p], sp_s.at[step, p], sp_r.at[step, p],
                      {"rows": lax.rem(r + p, R)})

    def stress(step):
        for c in range(NC):
            if step == 0:
                loads[c].wait()
            at = slice(c * W, c * W + W)

            def add(i, acc):
                tensor = [D[step, i, m, :, at] for m in range(3)]
                for m in range(3):
                    ES[step, 0, pl.ds(3 * i + m, 1), at] = tensor[m][0:1]
                    ES[step, 1, pl.ds(3 * i + m, 1), at] = tensor[m][15:16]
                spring = (1.0 + 2.0 / LMAX2) + (tensor[0] + tensor[2]) * (1.0 / LMAX2)
                return tuple(acc[m] + spring * tensor[m] for m in range(3))

            zero = jnp.zeros((16, W), jnp.float32)
            acc = lax.fori_loop(0, nf, add, (zero, zero, zero))
            acc = [one * (G_COEF / FIELDS) for one in acc]
            for m in range(3):
                ST[m, :, at] = acc[m]
            for m in (1, 2):
                row = (m - 1) * NC + c
                SES[step, 0, row:row + 1, :] = acc[m][0:1]
                SES[step, 1, row:row + 1, :] = acc[m][15:16]

    row16 = lax.broadcasted_iota(jnp.int32, (16, W), 0)

    def with_edges(rows, low, high):
        down, up = south_north(rows)
        return jnp.where(row16 == 0, low, down), jnp.where(row16 == 15, high, up)

    def force(step, c):
        at = slice(c * W, c * W + W)
        for comp in range(2):
            west, east = west_east(lambda lo, hi: ST[comp, :, lo:hi], c * W, W, NY)
            row = comp * NC + c
            down, up = with_edges(ST[comp + 1, :, at], SER[step, 0, row:row + 1, :], SER[step, 1, row:row + 1, :])
            FP[step, comp, :, at] = ((east - west) + (up - down)) * 0.5

    iota_cells = lax.broadcasted_iota(jnp.int32, (16, W), 0) * NY + lax.broadcasted_iota(jnp.int32, (16, W), 1)

    def noise(step, lo, hi):
        if hi <= lo:
            return

        def one(i, _):
            base = SD[i] * jnp.int32(2654435) + r * jnp.int32(16 * NY)
            for c in range(NC):
                for m in range(3):
                    h = iota_cells + (base + jnp.int32((3 * step + m) * 97531 + c * W))
                    h = jnp.bitwise_xor(h, lax.shift_right_logical(h, jnp.full_like(h, 16)))
                    h = h * jnp.int32(73244475)
                    h = jnp.bitwise_xor(h, lax.shift_right_logical(h, jnp.full_like(h, 16)))
                    h = h * jnp.int32(73244475)
                    h = jnp.bitwise_xor(h, lax.shift_right_logical(h, jnp.full_like(h, 16)))
                    h = jnp.bitwise_and(h, jnp.int32(65535)).astype(jnp.float32)
                    NZ[i, m, :, c * W:c * W + W] = h
            return 0

        lax.fori_loop(lo, hi, one, 0)

    def chain(step):
        def relay(i):
            @pl.when(not_end)
            def _():
                in_copy(step, i).wait_recv()
                at = slice(i * CW, i * CW + CW)
                FP[step, :, :, at] = FP[step, :, :, at] + CA[step, :, :, at]

        def spread(j, middle):
            at = slice(j * CW, j * CW + CW)
            mid_copy(step, j).wait_recv()
            total = CB[step, :, :, at]
            if middle:
                total = FP[step, :, :, at] + total
            TT[step, :, :, at] = total

            @pl.when(not_end)
            def _():
                total_copy(step, j).start()

            RH[step, :, 8:24, at] = FR[:, :, at] + total
            rh_copy(step, 0, j).start()
            rh_copy(step, 1, j).start()

        @pl.when(is_mid)
        def _():
            for i in range(K + LAG):
                if i < K:
                    relay(i)
                    mid_copy(step, i).start()
                    noise(step, i * nf // 16, (i + 1) * nf // 16)
                if i >= LAG:
                    spread(i - LAG, True)

        @pl.when(jnp.logical_not(is_mid))
        def _():
            for i in range(K):
                relay(i)
                in_copy(step, i).start()
            noise(step, 0, nf // 2)
            for j in range(K):
                spread(j, False)

    factor = 1.0 / (ALPHA + 4.0)

    NT = NY // 128

    def solve(step):
        row32 = lax.broadcasted_iota(jnp.int32, (32, 128), 0)
        for comp in range(2):
            for j, here, west, east in tiles_with_sides(
                lambda j: U32[step, comp, :, j * 128:j * 128 + 128], NT
            ):
                at = slice(j * 128, j * 128 + 128)
                row, part = comp * NC + j * 128 // W, j * 128 % W
                down, up = south_north(here)
                down = jnp.where(row32 == 0, XR[step, 0, row:row + 1, part:part + 128], down)
                up = jnp.where(row32 == 31, XR[step, 1, row:row + 1, part:part + 128], up)
                UU[1, comp, :, at] = (RH[step, comp, :, at] + ((up + down) + (east + west))) * factor

        def sweep(k, _):
            src, dst = lax.rem(k + 1, 2), lax.rem(k, 2)
            for comp in range(2):
                for j, here, west, east in tiles_with_sides(
                    lambda j: UU[src, comp, :, j * 128:j * 128 + 128], NT
                ):
                    at = slice(j * 128, j * 128 + 128)
                    down, up = south_north(here)
                    UU[dst, comp, :, at] = (RH[step, comp, :, at] + ((up + down) + (east + west))) * factor
            return 0

        lax.fori_loop(2, SWEEPS + 1, sweep, 0)

    def local_speed(step):
        top = None
        for c in range(NC):
            at = slice(c * W, c * W + W)
            one = jnp.abs(UU[0, 0, 8:24, at]) + jnp.abs(UU[0, 1, 8:24, at])
            one = jnp.maximum(one[0:8], one[8:16])
            for q in range(W // 128):
                part = one[:, q * 128:q * 128 + 128]
                top = part if top is None else jnp.maximum(top, part)
        SPR[step, 0] = top
        for p in range(1, R):
            sp_copy(step, p).start()

    def coefficients(step):
        top = SPR[step, 0]
        for p in range(1, R):
            sp_copy(step, p).wait_recv()
            top = jnp.maximum(top, SPR[step, p])
        top = jnp.max(jnp.max(top, axis=1, keepdims=True), axis=0, keepdims=True)
        dt = DT / (1.0 + top)
        loud = jnp.sqrt(dt) * (SIGMA / 18918.6)
        shift = loud * 32767.5
        for c in range(NC):
            at = slice(c * W, c * W + W)
            grads = []
            for comp in range(2):
                west, east = west_east(lambda lo, hi: UU[0, comp, 8:24, lo:hi], c * W, W, NY)
                down, up = south_north(UU[0, comp, :, at])
                grads.append((east - west) * 0.5)
                grads.append((up[8:24] - down[8:24]) * 0.5)
            lxx, lxy, lyx, lyy = [one * dt for one in grads]
            ux, uy = UU[0, 0, 8:24, at] * dt, UU[0, 1, 8:24, at] * dt
            centre = 1.0 - (jnp.abs(ux) + jnp.abs(uy)) - dt * ((1.0 + 2.0 / LMAX2) / LAMBDA)
            values = (
                jnp.maximum(ux, 0.0), -jnp.minimum(ux, 0.0), jnp.maximum(uy, 0.0), -jnp.minimum(uy, 0.0),
                centre + 2.0 * lxx, centre + (lxx + lyy), centre + 2.0 * lyy,
                lxy, lyx, (lxx + lxx) - shift, (lxy + lyx) - shift, (lyy + lyy) - shift,
            )
            for k, one in enumerate(values):
                COEF[k, :, at] = one
        return dt, loud

    row_a = lax.broadcasted_iota(jnp.int32, (16, 128), 0)

    def store_out(i):
        return pltpu.make_async_copy(D.at[0, i], out_d.at[i], out_sem.at[i])

    def advance(step, dt, loud):
        pull = jnp.broadcast_to(dt * (1.0 / (LMAX2 * LAMBDA)), (16, 128))
        loud = jnp.broadcast_to(loud, (16, 128))

        def one(i, _):
            def walk(m):
                return tiles_with_sides(lambda j: D[step, i, m, :, j * 128:j * 128 + 128], NT)

            for both in zip(walk(0), walk(1), walk(2)):
                j = both[0][0]
                at = slice(j * 128, j * 128 + 128)
                if j % 2 == 0:
                    pair = slice(j * 128, j * 128 + 256)
                    rims = [
                        [ER[step, side, pl.ds(3 * i + m, 1), pair] for m in range(3)] for side in range(2)
                    ]
                part = slice(j % 2 * 128, j % 2 * 128 + 128)
                a, b, d = [one[1] for one in both]
                q = (a + d) * pull
                xb, yb = COEF[7, :, at] * b, COEF[8, :, at] * b
                cross = (xb + xb, COEF[7, :, at] * d + COEF[8, :, at] * a, yb + yb)
                cw, ce, cs, cn = [COEF[k, :, at] for k in range(4)]
                for m, (_, x, west, east) in enumerate(both):
                    down, up = south_north(x)
                    down = jnp.where(row_a == 0, rims[0][m][:, part], down)
                    up = jnp.where(row_a == 15, rims[1][m][:, part], up)
                    fresh = (COEF[4 + m, :, at] - q) * x + cross[m]
                    fresh = fresh + (cw * west + ce * east)
                    fresh = fresh + (cs * down + cn * up)
                    D[1 - step, i, m, :, at] = fresh + (COEF[9 + m, :, at] + loud * NZ[i, m, :, at])
            if step == STEPS - 1:
                store_out(i).start()
            return 0

        lax.fori_loop(0, nf, one, 0)

    for step in range(STEPS):
        stress(step)
        if step == 0:
            pl.semaphore_wait(barrier, jnp.where(not_end, R + 1, R))
        for side in range(2):
            ses_copy(step, side).start()
        if step == 0:
            vel_load.wait()
            send_velocity(step)
            frc_load.wait()
            seed_load.wait()
        for side in range(2):
            es_copy(step, side).start()
        for side in range(2):
            ses_copy(step, side).wait_recv()
        for c in range(NC):
            force(step, c)
        chain(step)
        noise(step, nf // 2, 3 * nf // 4)
        for side in range(2):
            u_copy(step, side).wait_recv()
            x_copy(step, side).wait_recv()
            for c in range(K):
                rh_copy(step, side, c).wait_recv()
        solve(step)
        local_speed(step)
        if step < STEPS - 1:
            U32[step + 1, :, 8:24] = UU[0, :, 8:24]
            send_velocity(step + 1)
        else:
            out_u[...] = UU[0, :, 8:24]
        noise(step, 3 * nf // 4, nf)
        dt, loud = coefficients(step)
        for side in range(2):
            es_copy(step, side).wait_recv()
        advance(step, dt, loud)

    for step in range(STEPS):
        for side in range(2):
            ses_copy(step, side).wait_send()
            u_copy(step, side).wait_send()
            x_copy(step, side).wait_send()
            es_copy(step, side).wait_send()
        for c in range(K):
            in_copy(step, c).wait_send()
            rh_copy(step, 0, c).wait_send()
            rh_copy(step, 1, c).wait_send()
        for p in range(1, R):
            sp_copy(step, p).wait_send()

        @pl.when(not_end)
        def _():
            for c in range(K):
                total_copy(step, c).wait_send()

    def finish(i, _):
        store_out(i).wait()
        return 0

    lax.fori_loop(0, nf, finish, 0)


def body(R, F, deviation, seeds, velocity, forcing):
    nf, _, rows, NY = deviation.shape
    f32 = jnp.float32
    S = STEPS
    dma = pltpu.SemaphoreType.DMA
    vmem = lambda *shape: pltpu.VMEM(shape, f32)
    return pl.pallas_call(
        functools.partial(kernel, R, F),
        out_shape=(
            jax.ShapeDtypeStruct(deviation.shape, f32),
            jax.ShapeDtypeStruct(velocity.shape, f32),
        ),
        in_specs=[
            pl.BlockSpec(memory_space=pl.ANY),
            pl.BlockSpec(memory_space=pl.ANY),
            pl.BlockSpec(memory_space=pl.ANY),
            pl.BlockSpec(memory_space=pl.ANY),
        ],
        out_specs=(pl.BlockSpec(memory_space=pl.ANY), pl.BlockSpec(memory_space=pltpu.VMEM)),
        scratch_shapes=[
            vmem(2, nf, 3, rows, NY), vmem(nf, 3, rows, NY), vmem(3, rows, NY),
            vmem(S, 2, 8, 512), vmem(S, 2, 8, 512),
            vmem(S, 2, nf * 3, NY), vmem(S, 2, nf * 3, NY),
            vmem(S, 2, 32, NY), vmem(S, 2, 8, 512), vmem(S, 2, 8, 512),
            vmem(2, 2, 32, NY), vmem(S, 2, 32, NY), vmem(2, rows, NY), pltpu.SMEM((nf,), jnp.int32),
            vmem(S, 2, rows, NY), vmem(S, 2, rows, NY), vmem(S, 2, rows, NY), vmem(S, 2, rows, NY),
            vmem(12, rows, NY), vmem(S, R, 8, 128),
            dma((4,)), dma((3,)), dma((nf,)),
            *[dma((S, 2))] * 8,
            dma((S, K)), dma((S, K)), dma((S, K)), dma((S, K)),
            dma((S, 2, K)), dma((S, 2, K)), dma((S, R)), dma((S, R)),
        ],
        compiler_params=pltpu.CompilerParams(
            collective_id=0, has_side_effects=True, vmem_limit_bytes=63 * 1024 * 1024
        ),
    )(seeds, deviation, velocity, forcing)


def solution(mesh):
    return jax.shard_map(
        functools.partial(body, mesh.shape["rows"], mesh.shape["fields"]),
        mesh=mesh,
        in_specs=(
            P("fields", None, "rows", None),
            P("fields"),
            P(None, "rows", None),
            P(None, "rows", None),
        ),
        out_specs=(P("fields", None, "rows", None), P(None, "rows", None)),
        check_vma=False,
    )
```

```python
import functools

import jax
import jax.numpy as jnp
from jax import lax
from jax.experimental import pallas as pl
from jax.experimental.pallas import tpu as pltpu
from jax.sharding import PartitionSpec as P

FIELDS = 64
SWEEPS = 8
STEPS = 2

G_COEF = 4.0
ALPHA = 0.05
LMAX2 = 20.0
LAMBDA = 1.0
DT = 0.2
SIGMA = 1.0

K = 8
LAG = 3
MESH = pl.DeviceIdType.MESH


def widened(load, start, width, total):
    lo, hi = start - 128, start + width + 128
    if lo < 0:
        return jnp.concatenate([load(total + lo, total), load(0, hi)], axis=1)
    if hi > total:
        return jnp.concatenate([load(lo, total), load(0, hi - total)], axis=1)
    return load(lo, hi)


def west_east(load, start, width, total):
    wide = widened(load, start, width, total)
    span = width + 256
    west = pltpu.roll(wide, 1, 1)[:, 128:-128]
    east = pltpu.roll(wide, span - 1, 1)[:, 128:-128]
    return west, east


def tiles_with_sides(load, count):
    before = pltpu.roll(load(count - 1), 1, 1)
    here = load(0)
    here_w, here_e = pltpu.roll(here, 1, 1), pltpu.roll(here, 127, 1)
    lane = lax.broadcasted_iota(jnp.int32, here.shape, 1)
    first, last = lane == 0, lane == 127
    for j in range(count):
        after = load((j + 1) % count)
        after_w, after_e = pltpu.roll(after, 1, 1), pltpu.roll(after, 127, 1)
        yield j, here, jnp.where(first, before, here_w), jnp.where(last, after_e, here_e)
        before, here, here_w, here_e = here_w, after, after_w, after_e


def south_north(rows):
    count = rows.shape[0]
    return pltpu.roll(rows, 1, 0), pltpu.roll(rows, count - 1, 0)


def kernel(
    R, F, seeds_in, dev, vel, frc, out_d, out_u,
    D, NZ, ST, SES, SER, ES, ER, U32, XS, XR, UU, RH, FR, SD, FP, CA, CB, TT, COEF, SPR,
    in_sem, arg_sem, out_sem, ses_s, ses_r, u_s, u_r, x_s, x_r, es_s, es_r,
    in_s, a_r, b_r, t_s, rh_s, rh_r, sp_s, sp_r,
):
    nf, NY = dev.shape[0], dev.shape[3]
    r = lax.axis_index("rows")
    f = lax.axis_index("fields")
    south = {"rows": lax.rem(r + R - 1, R)}
    north = {"rows": lax.rem(r + 1, R)}
    half = F // 2
    is_low = f < half
    inward = {"fields": jnp.where(is_low, f + 1, f - 1)}
    outward_index = jnp.where(is_low, f - 1, f + 1)
    not_end = jnp.logical_and(f > 0, f < F - 1)
    is_mid = jnp.logical_or(f == half - 1, f == half)
    outward = {"fields": jnp.clip(outward_index, 0, F - 1)}
    CW = NY // K
    W = 512
    NC = NY // W

    def remote(src, dst, s, q, device):
        return pltpu.make_async_remote_copy(
            src_ref=src, dst_ref=dst, send_sem=s, recv_sem=q, device_id=device, device_id_type=MESH
        )

    loads = [
        pltpu.make_async_copy(
            dev.at[:, :, :, pl.ds(c * W, W)], D.at[0, :, :, :, pl.ds(c * W, W)], in_sem.at[c]
        )
        for c in range(NC)
    ]
    for one in loads:
        one.start()

    seed_load = pltpu.make_async_copy(seeds_in, SD, arg_sem.at[0])
    vel_load = pltpu.make_async_copy(vel, U32.at[0, :, pl.ds(8, 16)], arg_sem.at[1])
    frc_load = pltpu.make_async_copy(frc, FR, arg_sem.at[2])
    vel_load.start()
    frc_load.start()
    seed_load.start()
    barrier = pltpu.get_barrier_semaphore()
    for p in range(1, R):
        pl.semaphore_signal(barrier, inc=1, device_id={"rows": lax.rem(r + p, R)}, device_id_type=MESH)
    pl.semaphore_signal(barrier, inc=1, device_id=inward, device_id_type=MESH)

    @pl.when(not_end)
    def _():
        pl.semaphore_signal(barrier, inc=1, device_id=outward, device_id_type=MESH)

    def ses_copy(step, side, c):
        return remote(SES.at[step, side, c], SER.at[step, 1 - side, c], ses_s.at[step, side, c],
                      ses_r.at[step, 1 - side, c], south if side == 0 else north)

    def es_copy(step, side, h):
        return remote(ES.at[step, side, h], ER.at[step, 1 - side, h], es_s.at[step, side, h],
                      es_r.at[step, 1 - side, h], south if side == 0 else north)

    def u_copy(step, side):
        src = U32.at[step, :, pl.ds(8 if side == 0 else 16, 8)]
        dst = U32.at[step, :, pl.ds(24 if side == 0 else 0, 8)]
        return remote(src, dst, u_s.at[step, side], u_r.at[step, 1 - side], south if side == 0 else north)

    def x_copy(step, side):
        return remote(XS.at[step, side], XR.at[step, 1 - side], x_s.at[step, side],
                      x_r.at[step, 1 - side], south if side == 0 else north)

    def send_velocity(step):
        for comp in range(2):
            for c in range(NC):
                row = comp * NC + c
                at = slice(c * W, c * W + W)
                XS[step, 0, row:row + 1, :] = U32[step, comp, 16:24, at][0:1]
                XS[step, 1, row:row + 1, :] = U32[step, comp, 8:16, at][7:8]
        for side in range(2):
            u_copy(step, side).start()
            x_copy(step, side).start()

    def cols(c):
        return pl.ds(c * CW, CW)

    def in_copy(step, c):
        return remote(FP.at[step, :, :, cols(c)], CA.at[step, :, :, cols(c)], in_s.at[step, c],
                      a_r.at[step, c], inward)

    def mid_copy(step, c):
        return remote(FP.at[step, :, :, cols(c)], CB.at[step, :, :, cols(c)], in_s.at[step, c],
                      b_r.at[step, c], inward)

    def total_copy(step, c):
        return remote(TT.at[step, :, :, cols(c)], CB.at[step, :, :, cols(c)], t_s.at[step, c],
                      b_r.at[step, c], outward)

    def rh_copy(step, side, c):
        src = RH.at[step, :, pl.ds(8 if side == 0 else 16, 8), cols(c)]
        dst = RH.at[step, :, pl.ds(24 if side == 0 else 0, 8), cols(c)]
        return remote(src, dst, rh_s.at[step, side, c], rh_r.at[step, 1 - side, c],
                      south if side == 0 else north)

    def sp_copy(step, p):
        return remote(SPR.at[step, 0], SPR.at[step, p], sp_s.at[step, p], sp_r.at[step, p],
                      {"rows": lax.rem(r + p, R)})

    nh = nf // 2

    def stress(step, c):
        if step == 0:
            loads[c].wait()
        at = slice(c * W, c * W + W)
        zero = jnp.zeros((16, W), jnp.float32)
        acc = (zero, zero, zero)
        for h in range(2):
            def add(pair, acc):
                for q in range(2):
                    i = 2 * pair + q
                    tensor = [D[step, h * nh + i, m, :, at] for m in range(3)]
                    for m in range(3):
                        ES[step, 0, h, pl.ds(3 * i + m, 1), at] = tensor[m][0:1]
                        ES[step, 1, h, pl.ds(3 * i + m, 1), at] = tensor[m][15:16]
                    spring = (1.0 + 2.0 / LMAX2) + (tensor[0] + tensor[2]) * (1.0 / LMAX2)
                    acc = tuple(acc[m] + spring * tensor[m] for m in range(3))
                return acc

            acc = lax.fori_loop(0, nh // 2, add, acc)
        acc = [one * (G_COEF / FIELDS) for one in acc]
        for m in range(3):
            ST[m, :, at] = acc[m]
        for m in (1, 2):
            rows = slice(4 * m - 4, 4 * m)
            SES[step, 0, c, rows, :] = jnp.broadcast_to(acc[m][0:1], (4, W))
            SES[step, 1, c, rows, :] = jnp.broadcast_to(acc[m][15:16], (4, W))
        for side in range(2):
            ses_copy(step, side, c).start()

    row16 = lax.broadcasted_iota(jnp.int32, (16, W), 0)

    def with_edges(rows, low, high):
        down, up = south_north(rows)
        return jnp.where(row16 == 0, low, down), jnp.where(row16 == 15, high, up)

    def force(step, c):
        at = slice(c * W, c * W + W)
        for side in range(2):
            ses_copy(step, side, c).wait_recv()
        for comp in range(2):
            west, east = west_east(lambda lo, hi: ST[comp, :, lo:hi], c * W, W, NY)
            row = comp * 4
            down, up = with_edges(
                ST[comp + 1, :, at], SER[step, 0, c, row:row + 1, :], SER[step, 1, c, row:row + 1, :]
            )
            FP[step, comp, :, at] = ((east - west) + (up - down)) * 0.5

        @pl.when(jnp.logical_not(not_end))
        def _():
            for i in range(c * K // NC, (c + 1) * K // NC):
                (mid_copy if F == 2 else in_copy)(step, i).start()

    iota_cells = lax.broadcasted_iota(jnp.int32, (16, W), 0) * NY + lax.broadcasted_iota(jnp.int32, (16, W), 1)

    def noise(step, lo, hi):
        if hi <= lo:
            return

        def one(i, _):
            base = SD[i] * jnp.int32(2654435) + r * jnp.int32(16 * NY)
            for c in range(NC):
                for m in range(3):
                    h = iota_cells + (base + jnp.int32((3 * step + m) * 97531 + c * W))
                    h = jnp.bitwise_xor(h, lax.shift_right_logical(h, jnp.full_like(h, 16)))
                    h = h * jnp.int32(73244475)
                    h = jnp.bitwise_xor(h, lax.shift_right_logical(h, jnp.full_like(h, 16)))
                    h = h * jnp.int32(73244475)
                    h = jnp.bitwise_xor(h, lax.shift_right_logical(h, jnp.full_like(h, 16)))
                    h = jnp.bitwise_and(h, jnp.int32(65535)).astype(jnp.float32)
                    NZ[i, m, :, c * W:c * W + W] = h
            return 0

        lax.fori_loop(lo, hi, one, 0)

    order = [(i + K // NC) % K for i in range(K)]

    def chain(step):
        def relay(i, copy):
            @pl.when(not_end)
            def _():
                in_copy(step, i).wait_recv()
                at = slice(i * CW, i * CW + CW)
                FP[step, :, :, at] = FP[step, :, :, at] + CA[step, :, :, at]
                copy(step, i).start()

        def spread(j, middle):
            at = slice(j * CW, j * CW + CW)
            mid_copy(step, j).wait_recv()
            total = CB[step, :, :, at]
            if middle:
                total = FP[step, :, :, at] + total
            TT[step, :, :, at] = total

            @pl.when(not_end)
            def _():
                total_copy(step, j).start()

            RH[step, :, 8:24, at] = FR[:, :, at] + total
            rh_copy(step, 0, j).start()
            rh_copy(step, 1, j).start()

        @pl.when(is_mid)
        def _():
            for i in range(K + LAG):
                if i < K:
                    relay(order[i], mid_copy)
                    noise(step, i * nf // 16, (i + 1) * nf // 16)
                if i >= LAG:
                    spread(order[i - LAG], True)

        @pl.when(jnp.logical_not(is_mid))
        def _():
            for i in order:
                relay(i, in_copy)
            noise(step, 0, nf // 2)
            for j in order:
                spread(j, False)

    factor = 1.0 / (ALPHA + 4.0)

    NT = NY // 128

    def solve(step):
        row32 = lax.broadcasted_iota(jnp.int32, (32, 128), 0)
        for comp in range(2):
            for j, here, west, east in tiles_with_sides(
                lambda j: U32[step, comp, :, j * 128:j * 128 + 128], NT
            ):
                at = slice(j * 128, j * 128 + 128)
                row, part = comp * NC + j * 128 // W, j * 128 % W
                down, up = south_north(here)
                down = jnp.where(row32 == 0, XR[step, 0, row:row + 1, part:part + 128], down)
                up = jnp.where(row32 == 31, XR[step, 1, row:row + 1, part:part + 128], up)
                UU[1, comp, :, at] = (RH[step, comp, :, at] + ((up + down) + (east + west))) * factor

        def sweep(k, _):
            src, dst = lax.rem(k + 1, 2), lax.rem(k, 2)
            for comp in range(2):
                for j, here, west, east in tiles_with_sides(
                    lambda j: UU[src, comp, :, j * 128:j * 128 + 128], NT
                ):
                    at = slice(j * 128, j * 128 + 128)
                    down, up = south_north(here)
                    UU[dst, comp, :, at] = (RH[step, comp, :, at] + ((up + down) + (east + west))) * factor
            return 0

        lax.fori_loop(2, SWEEPS + 1, sweep, 0)

    def local_speed(step):
        top = None
        for c in range(NC):
            at = slice(c * W, c * W + W)
            one = jnp.abs(UU[0, 0, 8:24, at]) + jnp.abs(UU[0, 1, 8:24, at])
            one = jnp.maximum(one[0:8], one[8:16])
            for q in range(W // 128):
                part = one[:, q * 128:q * 128 + 128]
                top = part if top is None else jnp.maximum(top, part)
        SPR[step, 0] = top
        for p in range(1, R):
            sp_copy(step, p).start()

    def coefficients(step):
        top = SPR[step, 0]
        for p in range(1, R):
            sp_copy(step, p).wait_recv()
            top = jnp.maximum(top, SPR[step, p])
        top = jnp.max(jnp.max(top, axis=1, keepdims=True), axis=0, keepdims=True)
        dt = DT / (1.0 + top)
        loud = jnp.sqrt(dt) * (SIGMA / 18918.6)
        shift = loud * 32767.5
        for c in range(NC):
            at = slice(c * W, c * W + W)
            grads = []
            for comp in range(2):
                west, east = west_east(lambda lo, hi: UU[0, comp, 8:24, lo:hi], c * W, W, NY)
                down, up = south_north(UU[0, comp, :, at])
                grads.append((east - west) * 0.5)
                grads.append((up[8:24] - down[8:24]) * 0.5)
            lxx, lxy, lyx, lyy = [one * dt for one in grads]
            ux, uy = UU[0, 0, 8:24, at] * dt, UU[0, 1, 8:24, at] * dt
            centre = 1.0 - (jnp.abs(ux) + jnp.abs(uy)) - dt * ((1.0 + 2.0 / LMAX2) / LAMBDA)
            values = (
                jnp.maximum(ux, 0.0), -jnp.minimum(ux, 0.0), jnp.maximum(uy, 0.0), -jnp.minimum(uy, 0.0),
                centre + 2.0 * lxx, centre + (lxx + lyy), centre + 2.0 * lyy,
                lxy, lyx, (lxx + lxx) - shift, (lxy + lyx) - shift, (lyy + lyy) - shift,
            )
            for k, one in enumerate(values):
                COEF[k, :, at] = one
        return dt, loud

    row_a = lax.broadcasted_iota(jnp.int32, (16, 128), 0)

    def store_out(i):
        return pltpu.make_async_copy(D.at[0, i], out_d.at[i], out_sem.at[i])

    def advance(step, dt, loud, h):
        pull = jnp.broadcast_to(dt * (1.0 / (LMAX2 * LAMBDA)), (16, 128))
        loud = jnp.broadcast_to(loud, (16, 128))

        def one(k, _):
            i = h * nh + k

            def walk(m):
                return tiles_with_sides(lambda j: D[step, i, m, :, j * 128:j * 128 + 128], NT)

            for both in zip(walk(0), walk(1), walk(2)):
                j = both[0][0]
                at = slice(j * 128, j * 128 + 128)
                if j % 2 == 0:
                    pair = slice(j * 128, j * 128 + 256)
                    rims = [
                        [ER[step, side, h, pl.ds(3 * k + m, 1), pair] for m in range(3)] for side in range(2)
                    ]
                part = slice(j % 2 * 128, j % 2 * 128 + 128)
                a, b, d = [one[1] for one in both]
                q = (a + d) * pull
                xb, yb = COEF[7, :, at] * b, COEF[8, :, at] * b
                cross = (xb + xb, COEF[7, :, at] * d + COEF[8, :, at] * a, yb + yb)
                cw, ce, cs, cn = [COEF[n, :, at] for n in range(4)]
                for m, (_, x, west, east) in enumerate(both):
                    down, up = south_north(x)
                    down = jnp.where(row_a == 0, rims[0][m][:, part], down)
                    up = jnp.where(row_a == 15, rims[1][m][:, part], up)
                    fresh = (COEF[4 + m, :, at] - q) * x + cross[m]
                    fresh = fresh + (cw * west + ce * east)
                    fresh = fresh + (cs * down + cn * up)
                    D[1 - step, i, m, :, at] = fresh + (COEF[9 + m, :, at] + loud * NZ[i, m, :, at])
            if step == STEPS - 1:
                store_out(i).start()
            return 0

        lax.fori_loop(0, nh, one, 0)

    for step in range(STEPS):
        if step == 0:
            pl.semaphore_wait(barrier, jnp.where(not_end, R + 1, R))
        for c in range(NC):
            stress(step, c)
            if c >= 2:
                force(step, c - 1)
        force(step, NC - 1)
        force(step, 0)
        if step == 0:
            vel_load.wait()
            send_velocity(step)
            frc_load.wait()
            seed_load.wait()
        for side in range(2):
            es_copy(step, side, 0).start()
        chain(step)
        for side in range(2):
            es_copy(step, side, 1).start()
        noise(step, nf // 2, 3 * nf // 4)
        for side in range(2):
            u_copy(step, side).wait_recv()
            x_copy(step, side).wait_recv()
            for c in range(K):
                rh_copy(step, side, c).wait_recv()
        solve(step)
        local_speed(step)
        if step < STEPS - 1:
            U32[step + 1, :, 8:24] = UU[0, :, 8:24]
            send_velocity(step + 1)
        else:
            out_u[...] = UU[0, :, 8:24]
        noise(step, 3 * nf // 4, nf)
        dt, loud = coefficients(step)
        for h in range(2):
            for side in range(2):
                es_copy(step, side, h).wait_recv()
            advance(step, dt, loud, h)

    for step in range(STEPS):
        for side in range(2):
            for c in range(NC):
                ses_copy(step, side, c).wait_send()
            u_copy(step, side).wait_send()
            x_copy(step, side).wait_send()
            for h in range(2):
                es_copy(step, side, h).wait_send()
        for c in range(K):
            in_copy(step, c).wait_send()
            rh_copy(step, 0, c).wait_send()
            rh_copy(step, 1, c).wait_send()
        for p in range(1, R):
            sp_copy(step, p).wait_send()

        @pl.when(not_end)
        def _():
            for c in range(K):
                total_copy(step, c).wait_send()

    def finish(i, _):
        store_out(i).wait()
        return 0

    lax.fori_loop(0, nf, finish, 0)


def body(R, F, deviation, seeds, velocity, forcing):
    nf, _, rows, NY = deviation.shape
    f32 = jnp.float32
    S = STEPS
    dma = pltpu.SemaphoreType.DMA
    vmem = lambda *shape: pltpu.VMEM(shape, f32)
    return pl.pallas_call(
        functools.partial(kernel, R, F),
        out_shape=(
            jax.ShapeDtypeStruct(deviation.shape, f32),
            jax.ShapeDtypeStruct(velocity.shape, f32),
        ),
        in_specs=[
            pl.BlockSpec(memory_space=pl.ANY),
            pl.BlockSpec(memory_space=pl.ANY),
            pl.BlockSpec(memory_space=pl.ANY),
            pl.BlockSpec(memory_space=pl.ANY),
        ],
        out_specs=(pl.BlockSpec(memory_space=pl.ANY), pl.BlockSpec(memory_space=pltpu.VMEM)),
        scratch_shapes=[
            vmem(2, nf, 3, rows, NY), vmem(nf, 3, rows, NY), vmem(3, rows, NY),
            vmem(S, 2, NY // 512, 8, 512), vmem(S, 2, NY // 512, 8, 512),
            vmem(S, 2, 2, nf * 3 // 2, NY), vmem(S, 2, 2, nf * 3 // 2, NY),
            vmem(S, 2, 32, NY), vmem(S, 2, 8, 512), vmem(S, 2, 8, 512),
            vmem(2, 2, 32, NY), vmem(S, 2, 32, NY), vmem(2, rows, NY), pltpu.SMEM((nf,), jnp.int32),
            vmem(S, 2, rows, NY), vmem(S, 2, rows, NY), vmem(S, 2, rows, NY), vmem(S, 2, rows, NY),
            vmem(12, rows, NY), vmem(S, R, 8, 128),
            dma((4,)), dma((3,)), dma((nf,)),
            *[dma((S, 2, NY // 512))] * 2, *[dma((S, 2))] * 4, *[dma((S, 2, 2))] * 2,
            dma((S, K)), dma((S, K)), dma((S, K)), dma((S, K)),
            dma((S, 2, K)), dma((S, 2, K)), dma((S, R)), dma((S, R)),
        ],
        compiler_params=pltpu.CompilerParams(
            collective_id=0, has_side_effects=True, vmem_limit_bytes=63 * 1024 * 1024
        ),
    )(seeds, deviation, velocity, forcing)


def solution(mesh):
    return jax.shard_map(
        functools.partial(body, mesh.shape["rows"], mesh.shape["fields"]),
        mesh=mesh,
        in_specs=(
            P("fields", None, "rows", None),
            P("fields"),
            P(None, "rows", None),
            P(None, "rows", None),
        ),
        out_specs=(P("fields", None, "rows", None), P(None, "rows", None)),
        check_vma=False,
    )
```

```python
import functools

import jax
import jax.numpy as jnp
from jax import lax
from jax.experimental import pallas as pl
from jax.experimental.pallas import tpu as pltpu
from jax.sharding import PartitionSpec as P

FIELDS = 64
SWEEPS = 8
STEPS = 2

G_COEF = 4.0
ALPHA = 0.05
LMAX2 = 20.0
LAMBDA = 1.0
DT = 0.2
SIGMA = 1.0

K = 8
LAG = 3
MESH = pl.DeviceIdType.MESH


def widened(load, start, width, total):
    lo, hi = start - 128, start + width + 128
    if lo < 0:
        return jnp.concatenate([load(total + lo, total), load(0, hi)], axis=1)
    if hi > total:
        return jnp.concatenate([load(lo, total), load(0, hi - total)], axis=1)
    return load(lo, hi)


def west_east(load, start, width, total):
    wide = widened(load, start, width, total)
    span = width + 256
    west = pltpu.roll(wide, 1, 1)[:, 128:-128]
    east = pltpu.roll(wide, span - 1, 1)[:, 128:-128]
    return west, east


def tiles_with_sides(load, count):
    before = pltpu.roll(load(count - 1), 1, 1)
    here = load(0)
    here_w, here_e = pltpu.roll(here, 1, 1), pltpu.roll(here, 127, 1)
    lane = lax.broadcasted_iota(jnp.int32, here.shape, 1)
    first, last = lane == 0, lane == 127
    for j in range(count):
        after = load((j + 1) % count)
        after_w, after_e = pltpu.roll(after, 1, 1), pltpu.roll(after, 127, 1)
        yield j, here, jnp.where(first, before, here_w), jnp.where(last, after_e, here_e)
        before, here, here_w, here_e = here_w, after, after_w, after_e


def south_north(rows):
    count = rows.shape[0]
    return pltpu.roll(rows, 1, 0), pltpu.roll(rows, count - 1, 0)


def kernel(
    R, F, seeds_in, dev, vel, frc, out_d, out_u, out_root,
    D, NZ, ST, SES, SER, ES, ER, U32, XS, XR, UU, RH, FR, SD, FP, CA, CB, TT, COEF, SPR,
    in_sem, arg_sem, out_sem, ses_s, ses_r, u_s, u_r, x_s, x_r, es_s, es_r,
    in_s, a_r, b_r, t_s, rh_s, rh_r, sp_s, sp_r,
):
    nf, NY = dev.shape[0], dev.shape[3]
    r = lax.axis_index("rows")
    f = lax.axis_index("fields")
    south = {"rows": lax.rem(r + R - 1, R)}
    north = {"rows": lax.rem(r + 1, R)}
    half = F // 2
    is_low = f < half
    inward = {"fields": jnp.where(is_low, f + 1, f - 1)}
    outward_index = jnp.where(is_low, f - 1, f + 1)
    not_end = jnp.logical_and(f > 0, f < F - 1)
    is_mid = jnp.logical_or(f == half - 1, f == half)
    outward = {"fields": jnp.clip(outward_index, 0, F - 1)}
    CW = NY // K
    W = 512
    NC = NY // W

    def remote(src, dst, s, q, device):
        return pltpu.make_async_remote_copy(
            src_ref=src, dst_ref=dst, send_sem=s, recv_sem=q, device_id=device, device_id_type=MESH
        )

    loads = [
        pltpu.make_async_copy(
            dev.at[:, :, :, pl.ds(c * W, W)], D.at[0, :, :, :, pl.ds(c * W, W)], in_sem.at[c]
        )
        for c in range(NC)
    ]
    for one in loads:
        one.start()

    seed_load = pltpu.make_async_copy(seeds_in, SD, arg_sem.at[0])
    vel_load = pltpu.make_async_copy(vel, U32.at[0, :, pl.ds(8, 16)], arg_sem.at[1])
    frc_load = pltpu.make_async_copy(frc, FR, arg_sem.at[2])
    vel_load.start()
    frc_load.start()
    seed_load.start()
    barrier = pltpu.get_barrier_semaphore()
    for p in range(1, R):
        pl.semaphore_signal(barrier, inc=1, device_id={"rows": lax.rem(r + p, R)}, device_id_type=MESH)
    pl.semaphore_signal(barrier, inc=1, device_id=inward, device_id_type=MESH)

    @pl.when(not_end)
    def _():
        pl.semaphore_signal(barrier, inc=1, device_id=outward, device_id_type=MESH)

    def ses_copy(step, side, c):
        return remote(SES.at[step, side, c], SER.at[step, 1 - side, c], ses_s.at[step, side, c],
                      ses_r.at[step, 1 - side, c], south if side == 0 else north)

    def es_copy(step, side, h):
        return remote(ES.at[step, side, h], ER.at[step, 1 - side, h], es_s.at[step, side, h],
                      es_r.at[step, 1 - side, h], south if side == 0 else north)

    def u_copy(step, side):
        src = U32.at[step, :, pl.ds(8 if side == 0 else 16, 8)]
        dst = U32.at[step, :, pl.ds(24 if side == 0 else 0, 8)]
        return remote(src, dst, u_s.at[step, side], u_r.at[step, 1 - side], south if side == 0 else north)

    def x_copy(step, side):
        return remote(XS.at[step, side], XR.at[step, 1 - side], x_s.at[step, side],
                      x_r.at[step, 1 - side], south if side == 0 else north)

    def send_velocity(step):
        for comp in range(2):
            for c in range(NC):
                row = comp * NC + c
                at = slice(c * W, c * W + W)
                XS[step, 0, row:row + 1, :] = U32[step, comp, 16:24, at][0:1]
                XS[step, 1, row:row + 1, :] = U32[step, comp, 8:16, at][7:8]
        for side in range(2):
            u_copy(step, side).start()
            x_copy(step, side).start()

    def cols(c):
        return pl.ds(c * CW, CW)

    def in_copy(step, c):
        return remote(FP.at[step, :, :, cols(c)], CA.at[step, :, :, cols(c)], in_s.at[step, c],
                      a_r.at[step, c], inward)

    def mid_copy(step, c):
        return remote(FP.at[step, :, :, cols(c)], CB.at[step, :, :, cols(c)], in_s.at[step, c],
                      b_r.at[step, c], inward)

    def total_copy(step, c):
        return remote(TT.at[step, :, :, cols(c)], CB.at[step, :, :, cols(c)], t_s.at[step, c],
                      b_r.at[step, c], outward)

    def rh_copy(step, side, c):
        src = RH.at[step, :, pl.ds(8 if side == 0 else 16, 8), cols(c)]
        dst = RH.at[step, :, pl.ds(24 if side == 0 else 0, 8), cols(c)]
        return remote(src, dst, rh_s.at[step, side, c], rh_r.at[step, 1 - side, c],
                      south if side == 0 else north)

    def sp_copy(step, p):
        return remote(SPR.at[step, 0], SPR.at[step, p], sp_s.at[step, p], sp_r.at[step, p],
                      {"rows": lax.rem(r + p, R)})

    nh = nf // 2

    def stress(step, c):
        if step == 0:
            loads[c].wait()
        at = slice(c * W, c * W + W)
        zero = jnp.zeros((16, W), jnp.float32)
        acc = (zero, zero, zero)
        for h in range(2):
            def add(pair, acc):
                for q in range(2):
                    i = 2 * pair + q
                    tensor = [D[step, h * nh + i, m, :, at] for m in range(3)]
                    for m in range(3):
                        ES[step, 0, h, pl.ds(3 * i + m, 1), at] = tensor[m][0:1]
                        ES[step, 1, h, pl.ds(3 * i + m, 1), at] = tensor[m][15:16]
                    spring = (1.0 + 2.0 / LMAX2) + (tensor[0] + tensor[2]) * (1.0 / LMAX2)
                    acc = tuple(acc[m] + spring * tensor[m] for m in range(3))
                return acc

            acc = lax.fori_loop(0, nh // 2, add, acc)
        acc = [one * (G_COEF / FIELDS) for one in acc]
        for m in range(3):
            ST[m, :, at] = acc[m]
        for m in (1, 2):
            rows = slice(4 * m - 4, 4 * m)
            SES[step, 0, c, rows, :] = jnp.broadcast_to(acc[m][0:1], (4, W))
            SES[step, 1, c, rows, :] = jnp.broadcast_to(acc[m][15:16], (4, W))
        for side in range(2):
            ses_copy(step, side, c).start()

    row16 = lax.broadcasted_iota(jnp.int32, (16, W), 0)

    def with_edges(rows, low, high):
        down, up = south_north(rows)
        return jnp.where(row16 == 0, low, down), jnp.where(row16 == 15, high, up)

    def force(step, c):
        at = slice(c * W, c * W + W)
        for side in range(2):
            ses_copy(step, side, c).wait_recv()
        for comp in range(2):
            west, east = west_east(lambda lo, hi: ST[comp, :, lo:hi], c * W, W, NY)
            row = comp * 4
            down, up = with_edges(
                ST[comp + 1, :, at], SER[step, 0, c, row:row + 1, :], SER[step, 1, c, row:row + 1, :]
            )
            FP[step, comp, :, at] = ((east - west) + (up - down)) * 0.5

        @pl.when(jnp.logical_not(not_end))
        def _():
            for i in range(c * K // NC, (c + 1) * K // NC):
                (mid_copy if F == 2 else in_copy)(step, i).start()

    iota_cells = lax.broadcasted_iota(jnp.int32, (16, W), 0) * NY + lax.broadcasted_iota(jnp.int32, (16, W), 1)

    def noise(step, lo, hi):
        if hi <= lo or step == STEPS - 1:
            return

        def one(i, _):
            base = SD[i] * jnp.int32(2654435) + r * jnp.int32(16 * NY)
            for c in range(NC):
                for m in range(3):
                    h = iota_cells + (base + jnp.int32((3 * step + m) * 97531 + c * W))
                    h = jnp.bitwise_xor(h, lax.shift_right_logical(h, jnp.full_like(h, 16)))
                    h = h * jnp.int32(73244475)
                    h = jnp.bitwise_xor(h, lax.shift_right_logical(h, jnp.full_like(h, 16)))
                    h = h * jnp.int32(73244475)
                    h = jnp.bitwise_xor(h, lax.shift_right_logical(h, jnp.full_like(h, 16)))
                    h = jnp.bitwise_and(h, jnp.int32(65535)).astype(jnp.float32)
                    NZ[i, m, :, c * W:c * W + W] = h
            return 0

        lax.fori_loop(lo, hi, one, 0)

    order = [(i + K // NC) % K for i in range(K)]

    def chain(step):
        def relay(i, copy):
            @pl.when(not_end)
            def _():
                in_copy(step, i).wait_recv()
                at = slice(i * CW, i * CW + CW)
                FP[step, :, :, at] = FP[step, :, :, at] + CA[step, :, :, at]
                copy(step, i).start()

        def spread(j, middle):
            at = slice(j * CW, j * CW + CW)
            mid_copy(step, j).wait_recv()
            total = CB[step, :, :, at]
            if middle:
                total = FP[step, :, :, at] + total
            TT[step, :, :, at] = total

            @pl.when(not_end)
            def _():
                total_copy(step, j).start()

            RH[step, :, 8:24, at] = FR[:, :, at] + total
            rh_copy(step, 0, j).start()
            rh_copy(step, 1, j).start()

        @pl.when(is_mid)
        def _():
            for i in range(K + LAG):
                if i < K:
                    relay(order[i], mid_copy)
                    noise(step, i * nf // 16, (i + 1) * nf // 16)
                if i >= LAG:
                    spread(order[i - LAG], True)

        @pl.when(jnp.logical_not(is_mid))
        def _():
            for i in order:
                relay(i, in_copy)
            noise(step, 0, nf // 2)
            for j in order:
                spread(j, False)

    factor = 1.0 / (ALPHA + 4.0)

    NT = NY // 128

    def solve(step):
        row32 = lax.broadcasted_iota(jnp.int32, (32, 128), 0)
        for comp in range(2):
            for j, here, west, east in tiles_with_sides(
                lambda j: U32[step, comp, :, j * 128:j * 128 + 128], NT
            ):
                at = slice(j * 128, j * 128 + 128)
                row, part = comp * NC + j * 128 // W, j * 128 % W
                down, up = south_north(here)
                down = jnp.where(row32 == 0, XR[step, 0, row:row + 1, part:part + 128], down)
                up = jnp.where(row32 == 31, XR[step, 1, row:row + 1, part:part + 128], up)
                UU[1, comp, :, at] = (RH[step, comp, :, at] + ((up + down) + (east + west))) * factor

        def sweep(k, _):
            src, dst = lax.rem(k + 1, 2), lax.rem(k, 2)
            for comp in range(2):
                for j, here, west, east in tiles_with_sides(
                    lambda j: UU[src, comp, :, j * 128:j * 128 + 128], NT
                ):
                    at = slice(j * 128, j * 128 + 128)
                    down, up = south_north(here)
                    UU[dst, comp, :, at] = (RH[step, comp, :, at] + ((up + down) + (east + west))) * factor
            return 0

        lax.fori_loop(2, SWEEPS + 1, sweep, 0)

    def local_speed(step):
        top = None
        for c in range(NC):
            at = slice(c * W, c * W + W)
            one = jnp.abs(UU[0, 0, 8:24, at]) + jnp.abs(UU[0, 1, 8:24, at])
            one = jnp.maximum(one[0:8], one[8:16])
            for q in range(W // 128):
                part = one[:, q * 128:q * 128 + 128]
                top = part if top is None else jnp.maximum(top, part)
        SPR[step, 0] = top
        for p in range(1, R):
            sp_copy(step, p).start()

    def coefficients(step):
        top = SPR[step, 0]
        for p in range(1, R):
            sp_copy(step, p).wait_recv()
            top = jnp.maximum(top, SPR[step, p])
        top = jnp.max(jnp.max(top, axis=1, keepdims=True), axis=0, keepdims=True)
        dt = DT / (1.0 + top)
        loud = jnp.sqrt(dt) * (SIGMA / 18918.6)
        shift = loud * 32767.5
        if step == STEPS - 1:
            out_root[...] = jnp.broadcast_to(jnp.sqrt(dt) * SIGMA, (8, 128))
            shift = 0.0
        for c in range(NC):
            at = slice(c * W, c * W + W)
            grads = []
            for comp in range(2):
                west, east = west_east(lambda lo, hi: UU[0, comp, 8:24, lo:hi], c * W, W, NY)
                down, up = south_north(UU[0, comp, :, at])
                grads.append((east - west) * 0.5)
                grads.append((up[8:24] - down[8:24]) * 0.5)
            lxx, lxy, lyx, lyy = [one * dt for one in grads]
            ux, uy = UU[0, 0, 8:24, at] * dt, UU[0, 1, 8:24, at] * dt
            centre = 1.0 - (jnp.abs(ux) + jnp.abs(uy)) - dt * ((1.0 + 2.0 / LMAX2) / LAMBDA)
            values = (
                jnp.maximum(ux, 0.0), -jnp.minimum(ux, 0.0), jnp.maximum(uy, 0.0), -jnp.minimum(uy, 0.0),
                centre + 2.0 * lxx, centre + (lxx + lyy), centre + 2.0 * lyy,
                lxy, lyx, (lxx + lxx) - shift, (lxy + lyx) - shift, (lyy + lyy) - shift,
            )
            for k, one in enumerate(values):
                COEF[k, :, at] = one
        return dt, loud

    row_a = lax.broadcasted_iota(jnp.int32, (16, 128), 0)

    def store_out(i):
        return pltpu.make_async_copy(D.at[0, i], out_d.at[i], out_sem.at[i])

    def advance(step, dt, loud, h):
        pull = jnp.broadcast_to(dt * (1.0 / (LMAX2 * LAMBDA)), (16, 128))
        loud = jnp.broadcast_to(loud, (16, 128))

        def one(k, _):
            i = h * nh + k

            def walk(m):
                return tiles_with_sides(lambda j: D[step, i, m, :, j * 128:j * 128 + 128], NT)

            for both in zip(walk(0), walk(1), walk(2)):
                j = both[0][0]
                at = slice(j * 128, j * 128 + 128)
                if j % 2 == 0:
                    pair = slice(j * 128, j * 128 + 256)
                    rims = [
                        [ER[step, side, h, pl.ds(3 * k + m, 1), pair] for m in range(3)] for side in range(2)
                    ]
                part = slice(j % 2 * 128, j % 2 * 128 + 128)
                a, b, d = [one[1] for one in both]
                q = (a + d) * pull
                xb, yb = COEF[7, :, at] * b, COEF[8, :, at] * b
                cross = (xb + xb, COEF[7, :, at] * d + COEF[8, :, at] * a, yb + yb)
                cw, ce, cs, cn = [COEF[n, :, at] for n in range(4)]
                for m, (_, x, west, east) in enumerate(both):
                    down, up = south_north(x)
                    down = jnp.where(row_a == 0, rims[0][m][:, part], down)
                    up = jnp.where(row_a == 15, rims[1][m][:, part], up)
                    fresh = (COEF[4 + m, :, at] - q) * x + cross[m]
                    fresh = fresh + (cw * west + ce * east)
                    fresh = fresh + (cs * down + cn * up)
                    fixed = COEF[9 + m, :, at]
                    if step < STEPS - 1:
                        fixed = fixed + loud * NZ[i, m, :, at]
                    D[1 - step, i, m, :, at] = fresh + fixed
            if step == STEPS - 1:
                store_out(i).start()
            return 0

        lax.fori_loop(0, nh, one, 0)

    for step in range(STEPS):
        if step == 0:
            pl.semaphore_wait(barrier, jnp.where(not_end, R + 1, R))
        for c in range(NC):
            stress(step, c)
            if c >= 2:
                force(step, c - 1)
        force(step, NC - 1)
        force(step, 0)
        if step == 0:
            vel_load.wait()
            send_velocity(step)
            frc_load.wait()
            seed_load.wait()
        for side in range(2):
            es_copy(step, side, 0).start()
        chain(step)
        for side in range(2):
            es_copy(step, side, 1).start()
        noise(step, nf // 2, 3 * nf // 4)
        for side in range(2):
            u_copy(step, side).wait_recv()
            x_copy(step, side).wait_recv()
            for c in range(K):
                rh_copy(step, side, c).wait_recv()
        solve(step)
        local_speed(step)
        if step < STEPS - 1:
            U32[step + 1, :, 8:24] = UU[0, :, 8:24]
            send_velocity(step + 1)
        else:
            out_u[...] = UU[0, :, 8:24]
        noise(step, 3 * nf // 4, nf)
        dt, loud = coefficients(step)
        for h in range(2):
            for side in range(2):
                es_copy(step, side, h).wait_recv()
            advance(step, dt, loud, h)

    for step in range(STEPS):
        for side in range(2):
            for c in range(NC):
                ses_copy(step, side, c).wait_send()
            u_copy(step, side).wait_send()
            x_copy(step, side).wait_send()
            for h in range(2):
                es_copy(step, side, h).wait_send()
        for c in range(K):
            in_copy(step, c).wait_send()
            rh_copy(step, 0, c).wait_send()
            rh_copy(step, 1, c).wait_send()
        for p in range(1, R):
            sp_copy(step, p).wait_send()

        @pl.when(not_end)
        def _():
            for c in range(K):
                total_copy(step, c).wait_send()

    def finish(i, _):
        store_out(i).wait()
        return 0

    lax.fori_loop(0, nf, finish, 0)


def last_noise(seeds, shape):
    iota = lambda dim: lax.broadcasted_iota(jnp.int32, shape, dim)
    _, _, rows, NY = shape
    h = (seeds * jnp.int32(2654435))[:, None, None, None] + (3 * (STEPS - 1) + iota(1)) * 97531
    h = h + ((lax.axis_index("rows") * rows + iota(2)) * NY + iota(3))
    h = jnp.bitwise_xor(h, lax.shift_right_logical(h, jnp.int32(16)))
    h = h * jnp.int32(73244475)
    h = jnp.bitwise_xor(h, lax.shift_right_logical(h, jnp.int32(16)))
    h = h * jnp.int32(73244475)
    h = jnp.bitwise_xor(h, lax.shift_right_logical(h, jnp.int32(16)))
    return (jnp.bitwise_and(h, jnp.int32(65535)).astype(jnp.float32) - 32767.5) * (1.0 / 18918.6)


def body(R, F, deviation, seeds, velocity, forcing):
    nf, _, rows, NY = deviation.shape
    f32 = jnp.float32
    S = STEPS
    dma = pltpu.SemaphoreType.DMA
    vmem = lambda *shape: pltpu.VMEM(shape, f32)
    fields, speed, root = pl.pallas_call(
        functools.partial(kernel, R, F),
        out_shape=(
            jax.ShapeDtypeStruct(deviation.shape, f32),
            jax.ShapeDtypeStruct(velocity.shape, f32),
            jax.ShapeDtypeStruct((8, 128), f32),
        ),
        in_specs=[
            pl.BlockSpec(memory_space=pl.ANY),
            pl.BlockSpec(memory_space=pl.ANY),
            pl.BlockSpec(memory_space=pl.ANY),
            pl.BlockSpec(memory_space=pl.ANY),
        ],
        out_specs=(
            pl.BlockSpec(memory_space=pl.ANY),
            pl.BlockSpec(memory_space=pltpu.VMEM),
            pl.BlockSpec(memory_space=pltpu.VMEM),
        ),
        scratch_shapes=[
            vmem(2, nf, 3, rows, NY), vmem(nf, 3, rows, NY), vmem(3, rows, NY),
            vmem(S, 2, NY // 512, 8, 512), vmem(S, 2, NY // 512, 8, 512),
            vmem(S, 2, 2, nf * 3 // 2, NY), vmem(S, 2, 2, nf * 3 // 2, NY),
            vmem(S, 2, 32, NY), vmem(S, 2, 8, 512), vmem(S, 2, 8, 512),
            vmem(2, 2, 32, NY), vmem(S, 2, 32, NY), vmem(2, rows, NY), pltpu.SMEM((nf,), jnp.int32),
            vmem(S, 2, rows, NY), vmem(S, 2, rows, NY), vmem(S, 2, rows, NY), vmem(S, 2, rows, NY),
            vmem(12, rows, NY), vmem(S, R, 8, 128),
            dma((4,)), dma((3,)), dma((nf,)),
            *[dma((S, 2, NY // 512))] * 2, *[dma((S, 2))] * 4, *[dma((S, 2, 2))] * 2,
            dma((S, K)), dma((S, K)), dma((S, K)), dma((S, K)),
            dma((S, 2, K)), dma((S, 2, K)), dma((S, R)), dma((S, R)),
        ],
        compiler_params=pltpu.CompilerParams(
            collective_id=0, has_side_effects=True, vmem_limit_bytes=63 * 1024 * 1024
        ),
    )(seeds, deviation, velocity, forcing)
    return fields + root[0, 0] * last_noise(seeds, deviation.shape), speed


def solution(mesh):
    return jax.shard_map(
        functools.partial(body, mesh.shape["rows"], mesh.shape["fields"]),
        mesh=mesh,
        in_specs=(
            P("fields", None, "rows", None),
            P("fields"),
            P(None, "rows", None),
            P(None, "rows", None),
        ),
        out_specs=(P("fields", None, "rows", None), P(None, "rows", None)),
        check_vma=False,
    )
```
